32 devices in a mesh: frames: 8 (over z, core), rows: 4 (over y, x).
Axes of the slice: x: 2, y: 2, z: 4, core: 2. Of those that a mesh axis runs over, the one named last changes fastest.
Arguments:
- images: float32 [16, 8, 96, 128], P('frames', 'rows'), may hold values from -6 to 6
- spatial_weight: float32 [3, 3, 128, 128], replicated, may hold values from -0.1875 to 0.1875
- temporal_weight: float32 [3, 128, 128], replicated, may hold values from -0.3125 to 0.3125
- cotangent: float32 [16, 8, 96, 128], P('frames', 'rows'), may hold values from -6 to 6
Outputs:
- block_out: float32 [16, 8, 96, 128], P('frames', 'rows')
- grad_images: float32 [16, 8, 96, 128], P('frames', 'rows')
- grad_spatial: float32 [3, 3, 128, 128], P(None, None, None, 'rows')
- grad_temporal: float32 [3, 128, 128], P(None, None, 'rows')
The draws below stay inside these ranges and needn't reach their ends.
All inputs are finite; a program needn't handle non-finite values.
Results may differ from the reference program's by a relative error of at most 0.0003.
Values sent between devices are 32-bit elements; how exact they have to be, the bound alone decides.
A program may use at most 64 MiB of HBM per device.

```python
import math
import jax
import jax.numpy as jnp
from jax import lax

C = 128
W = 96
FRAMES = 16
HEIGHT = 8


def shard_levels(own_key, dims, split, low, high):
    def one(position, shards_of):
        steps = jax.random.uniform(jax.random.fold_in(jax.random.fold_in(own_key, 6), position), (shards_of,), jnp.float32, low / len(split), high / len(split))
        return jnp.repeat(jnp.exp(steps), dims[position] // shards_of).reshape((-1,) + (1,) * (len(dims) - position - 1))

    factor_of = one(*split[0])
    for cut in split[1:]:
        factor_of = factor_of * one(*cut)
    return factor_of


def centred(own_key, dims, deviation, most, pieces=(), kind=jnp.bfloat16):
    result = deviation * jax.random.normal(own_key, dims, jnp.float32)
    if pieces:
        result = result * shard_levels(own_key, dims, pieces, -0.22, 0.18)
    return jnp.clip(result, -most, most).astype(kind)


def setup_inputs(seed: int = 0) -> dict:
    keys = jax.random.split(jax.random.key(seed), 5)
    images = centred(keys[0], (FRAMES, HEIGHT, W, C), 1.0, 6.0, ((0, 8), (1, 4)), jnp.float32)
    spatial_weight = centred(keys[1], (3, 3, C, C), (9 * C) ** -0.5, 0.1875, (), jnp.float32)
    temporal_weight = centred(keys[2], (3, C, C), (3 * C) ** -0.5, 0.3125, (), jnp.float32)
    cotangent = centred(keys[3], (FRAMES, HEIGHT, W, C), 1.0, 6.0, ((0, 8), (1, 4)), jnp.float32)
    return {"images": images, "spatial_weight": spatial_weight, "temporal_weight": temporal_weight, "cotangent": cotangent}


HIGH = lax.Precision.HIGHEST

def spatial(frame, kernel):
    height, width = (frame.shape[0], frame.shape[1])
    padded = jnp.pad(frame, ((1, 1), (1, 1), (0, 0)))
    total = jnp.zeros(frame.shape, jnp.float32)
    for i in range(3):
        for j in range(3):
            total = total + jnp.einsum('hwc,cd->hwd', padded[i:i + height, j:j + width], kernel[i, j], precision=HIGH)
    return total

def spatial_back(grad, kernel):
    height, width = (grad.shape[0], grad.shape[1])
    padded = jnp.pad(grad, ((1, 1), (1, 1), (0, 0)))
    total = jnp.zeros(grad.shape, jnp.float32)
    for i in range(3):
        for j in range(3):
            total = total + jnp.einsum('hwd,cd->hwc', padded[2 - i:2 - i + height, 2 - j:2 - j + width], kernel[i, j], precision=HIGH)
    return total

def kernel_terms(frame, grad):
    height, width = (frame.shape[0], frame.shape[1])
    padded = jnp.pad(frame, ((1, 1), (1, 1), (0, 0)))
    rows_out = []
    for i in range(3):
        cols_out = []
        for j in range(3):
            cols_out.append(jnp.einsum('hwc,hwd->cd', padded[i:i + height, j:j + width], grad, precision=HIGH))
        rows_out.append(jnp.stack(cols_out))
    return jnp.stack(rows_out)

def reference(images, spatial_weight, temporal_weight, cotangent):
    nframes, height, width, chans = images.shape
    pre = lax.map(lambda frame: spatial(frame, spatial_weight), images)

    def fetch(array, index):
        safe = jnp.clip(index, 0, nframes - 1).astype(jnp.int32)
        valid = jnp.logical_and(index >= 0, index < nframes)
        return jnp.where(valid, lax.dynamic_index_in_dim(array, safe, 0, keepdims=False), jnp.zeros((height, width, chans), jnp.float32))

    def activ(value):
        return value * jax.nn.sigmoid(value)

    def step(carry, index):
        acc_s, acc_t = carry
        pre_now = fetch(pre, index)
        sig = jax.nn.sigmoid(pre_now)
        lagged = [activ(pre_now), activ(fetch(pre, index - 1)), activ(fetch(pre, index - 2))]
        grads = [fetch(cotangent, index), fetch(cotangent, index + 1), fetch(cotangent, index + 2)]
        mixed = jnp.zeros((height, width, chans), jnp.float32)
        dact = jnp.zeros((height, width, chans), jnp.float32)
        for k in range(3):
            mixed = mixed + jnp.einsum('hwc,cd->hwd', lagged[k], temporal_weight[k], precision=HIGH)
            dact = dact + jnp.einsum('hwd,cd->hwc', grads[k], temporal_weight[k], precision=HIGH)
        out_now = fetch(images, index) + mixed
        dpre = dact * sig * (1.0 + pre_now * (1.0 - sig))
        gimg = grads[0] + spatial_back(dpre, spatial_weight)
        acc_s = acc_s + kernel_terms(fetch(images, index), dpre)
        acc_t = acc_t + jnp.stack([jnp.einsum('hwc,hwd->cd', lagged[k], grads[0], precision=HIGH) for k in range(3)])
        return ((acc_s, acc_t), (out_now, gimg))
    start = (jnp.zeros((3, 3, chans, chans), jnp.float32), jnp.zeros((3, chans, chans), jnp.float32))
    (acc_s, acc_t), (block_out, grad_images) = lax.scan(step, start, jnp.arange(nframes, dtype=jnp.int32))
    factor = 1.0 / math.sqrt(nframes * height * width)
    return (block_out, grad_images, acc_s * factor, acc_t * factor)
```

```python
import functools
import math

import jax
import jax.numpy as jnp
from jax import lax
from jax.experimental import pallas as pl
from jax.experimental.pallas import tpu as pltpu
from jax.sharding import PartitionSpec as P

MESH = pl.DeviceIdType.MESH
F32, BF16 = jnp.float32, jnp.bfloat16
GROUPS = 2


def split(value):
    high = value.astype(BF16)
    return high, (value - high.astype(F32)).astype(BF16)


def dot(a, b):
    return jnp.dot(a, b, preferred_element_type=F32)


def put_weight(dst, index, value):
    high, low = split(value)
    n = value.shape[1]
    dst[index, :, :n] = high
    dst[index, :, n:] = low


def product(high, low, both):
    n = both.shape[1] // 2
    wide = dot(high, both)
    return wide[:, :n] + wide[:, n:] + dot(low, both[:, :n])


def put_row(dst, row, frames):
    width, chans = frames[0].shape
    at = lax.broadcasted_iota(jnp.int32, (width, chans), 0)
    for f, value in enumerate(frames):
        before = jnp.where(at == 0, 0.0, pltpu.roll(value, 1, 0))
        after = jnp.where(at == width - 1, 0.0, pltpu.roll(value, width - 1, 0))
        rows = pl.ds(f * width, width)
        for b, moved in enumerate((before, value, after)):
            high, low = split(moved)
            dst[row, rows, b * chans : (b + 1) * chans] = high
            dst[row, rows, (3 + b) * chans : (4 + b) * chans] = low


def kernel(
    nfd, nrd, share, piece, factor,
    x_ref, sw_ref, tw_ref, cot_ref, mix_ref, gi_ref, gr_ref,
    xs, ds, wf, wb, tf, tb, xhalo, chalo, ahalo, dhalo, act, dpre, cots, acts,
    terms, core_in, half, rows_in, plane, z_in, own, final, send_sem, recv_sem,
):
    nf, strip, width, chans = x_ref.shape
    assert nf == 2 and strip == 2
    wide = nf * width
    three = 3 * chans
    fr, ro = lax.axis_index("frames"), lax.axis_index("rows")
    core, z = lax.rem(fr, 2), lax.div(fr, 2)
    nz = nfd // 2
    other = fr + 1 - 2 * core
    n_sems = [0]
    sent = []

    def remote(src, dst, **where):
        n = n_sems[0]
        n_sems[0] += 1
        return pltpu.make_async_remote_copy(
            src_ref=src, dst_ref=dst, send_sem=send_sem.at[n], recv_sem=recv_sem.at[n],
            device_id=where, device_id_type=MESH,
        )

    def send(src, dst, **where):
        copy = remote(src, dst, **where)
        copy.start()
        sent.append(copy)
        return copy

    barrier = pltpu.get_barrier_semaphore()
    for o in range(1, nrd):
        pl.semaphore_signal(barrier, inc=1, device_id={"rows": lax.rem(ro + o, nrd)}, device_id_type=MESH)
    for o in range(1, nfd):
        pl.semaphore_signal(barrier, inc=1, device_id={"frames": lax.rem(fr + o, nfd)}, device_id_type=MESH)

    for h in range(strip):
        put_row(xs, h + 1, [x_ref[f, h] for f in range(nf)])

    pl.semaphore_wait(barrier, nrd - 1 + nfd - 1)

    has_up, has_down = ro > 0, ro < nrd - 1
    has_prev, has_next = fr > 0, fr < nfd - 1
    up, down = lax.rem(ro + nrd - 1, nrd), lax.rem(ro + 1, nrd)
    prev, following = lax.rem(fr + nfd - 1, nfd), lax.rem(fr + 1, nfd)
    x_up = remote(x_ref.at[:, 0], xhalo.at[1], rows=up)
    x_down = remote(x_ref.at[:, strip - 1], xhalo.at[0], rows=down)
    c_prev = remote(cot_ref, chalo, frames=prev)
    a_next = remote(act, ahalo, frames=following)
    d_up = remote(dpre.at[0], dhalo.at[1], rows=up)
    d_down = remote(dpre.at[strip - 1], dhalo.at[0], rows=down)

    def receive(copy, there, zeroed):
        @pl.when(there)
        def _():
            copy.wait_recv()

        @pl.when(jnp.logical_not(there))
        def _():
            zeroed[...] = jnp.zeros(zeroed.shape, F32)

    @pl.when(has_up)
    def _():
        x_up.start()

    @pl.when(has_down)
    def _():
        x_down.start()

    @pl.when(has_prev)
    def _():
        c_prev.start()

    for i in range(3):
        put_weight(wf, i, sw_ref[i].reshape(three, chans))
    for k in range(3):
        put_weight(tb, k, tw_ref[k].T)
        put_weight(tf, k, tw_ref[k])
    for f in range(nf):
        for h in range(strip):
            high, low = split(cot_ref[f, h])
            cots[0, h, pl.ds(f * width, width), :] = high
            cots[1, h, pl.ds(f * width, width), :] = low

    def conv(src, row, weight, i):
        return product(src[row, :, :three], src[row, :, three:], weight[i])

    pre = [conv(xs, 1, wf, 1) + conv(xs, 2, wf, 2), conv(xs, 1, wf, 0) + conv(xs, 2, wf, 1)]
    for i in range(3):
        put_weight(wb, i, jnp.concatenate([sw_ref[i, 2 - b].T for b in range(3)], axis=0))

    receive(x_down, has_up, xhalo.at[0])
    receive(x_up, has_down, xhalo.at[1])
    put_row(xs, 0, [xhalo[0, f] for f in range(nf)])
    put_row(xs, 3, [xhalo[1, f] for f in range(nf)])
    pre = [pre[0] + conv(xs, 0, wf, 0), pre[1] + conv(xs, 3, wf, 2)]
    receive(c_prev, has_next, chalo)
    for f in range(nf):
        for h in range(strip):
            high, low = split(chalo[f, h])
            cots[0, h, pl.ds(wide + f * width, width), :] = high
            cots[1, h, pl.ds(wide + f * width, width), :] = low

    both_act, both_dpre = [], []
    for h in range(strip):
        sig = 1.0 / (1.0 + jnp.exp(-pre[h]))
        act_h = pre[h] * sig
        act[h] = act_h
        dact = None
        for k in range(3):
            rows = pl.ds(k * width, wide)
            term = product(cots[0, h, rows, :], cots[1, h, rows, :], tb[k])
            dact = term if dact is None else dact + term
        dpre_h = dact * sig * (1.0 + pre[h] * (1.0 - sig))
        dpre[h] = dpre_h
        both_act.append(act_h)
        both_dpre.append(dpre_h)

    @pl.when(has_up)
    def _():
        d_up.start()

    @pl.when(has_down)
    def _():
        d_down.start()

    @pl.when(has_next)
    def _():
        a_next.start()

    act_t = split(jnp.concatenate(both_act, axis=0).T)
    for k in range(3):
        rows = pl.ds(k * width, wide)
        c_high = cots[0, :, rows, :].reshape(strip * wide, chans)
        c_low = cots[1, :, rows, :].reshape(strip * wide, chans)
        term = dot(act_t[0], c_high) + dot(act_t[0], c_low) + dot(act_t[1], c_high)
        terms[0, 0, k] = term.T
    dpre_t = split(jnp.concatenate(both_dpre, axis=0).T)

    def spatial_terms(i, g, side):
        src = xs[i : i + strip].reshape(strip * wide, 2 * three)
        wide_term = dot(dpre_t[0], src)
        term = wide_term[:, :three] + wide_term[:, three:] + dot(dpre_t[1], src[:, :three])
        for j in range(3):
            terms[g, side, j] = term[:, j * chans : (j + 1) * chans]

    spatial_terms(0, 0, 1)
    to_core = [None] * GROUPS
    to_rows = [None] * GROUPS
    to_z = [None] * GROUPS
    around_z = [None] * GROUPS
    back = [None] * GROUPS

    def start_core(g):
        to_core[g] = send(terms.at[g, 1 - core], core_in.at[g], frames=other)

    def start_rows(g):
        to_core[g].wait_recv()
        half[g] = terms[g, core] + core_in[g]
        to_rows[g] = []
        for o in range(1, nrd):
            target = lax.rem(ro + o, nrd)
            part = pl.ds(pl.multiple_of(target * share, 8), share)
            to_rows[g].append(send(half.at[g, :, part, :], rows_in.at[g, o - 1], rows=target))

    def start_z(g):
        total = half[g, :, pl.ds(pl.multiple_of(ro * share, 8), share), :]
        for o in range(1, nrd):
            to_rows[g][o - 1].wait_recv()
            total = total + rows_in[g, o - 1]
        plane[g, : 3 * share] = total.reshape(3 * share, chans) * factor
        if nz * piece > 3 * share:
            plane[g, 3 * share :] = jnp.zeros((nz * piece - 3 * share, chans), F32)
        to_z[g] = []
        for o in range(1, nz):
            target = lax.rem(z + o, nz)
            part = pl.ds(pl.multiple_of(target * piece, 8), piece)
            to_z[g].append(send(plane.at[g, part], z_in.at[g, o - 1], frames=2 * target + core))

    def start_around(g):
        mine = pl.ds(pl.multiple_of(z * piece, 8), piece)
        total = plane[g, mine]
        for o in range(1, nz):
            to_z[g][o - 1].wait_recv()
            total = total + z_in[g, o - 1]
        own[g, 0] = total
        final[g, core, mine] = total
        around_z[g] = []
        for o in range(1, nz):
            target = lax.rem(z + o, nz)
            around_z[g].append(send(own.at[g, 0], final.at[g, core, mine], frames=2 * target + core))

    def start_back(g):
        for copy in around_z[g]:
            copy.wait_recv()
        back[g] = send(final.at[g, core], final.at[g, core], frames=other)

    def finish(g):
        back[g].wait_recv()
        gr_ref[g] = final[g]

    def mixed():
        receive(a_next, has_prev, ahalo)
        for h in range(strip):
            for part, value in ((0, ahalo[h]), (1, act[h])):
                high, low = split(value)
                acts[0, h, pl.ds(part * wide, wide), :] = high
                acts[1, h, pl.ds(part * wide, wide), :] = low
        for h in range(strip):
            total = None
            for k in range(3):
                rows = pl.ds((2 - k) * width, wide)
                term = product(acts[0, h, rows, :], acts[1, h, rows, :], tf[k])
                total = term if total is None else total + term
            for f in range(nf):
                mix_ref[f, h] = total[f * width : (f + 1) * width]

    def image_gradient():
        receive(d_down, has_up, dhalo.at[0])
        receive(d_up, has_down, dhalo.at[1])
        put_row(ds, 0, [dhalo[0, pl.ds(f * width, width)] for f in range(nf)])
        put_row(ds, 3, [dhalo[1, pl.ds(f * width, width)] for f in range(nf)])
        for h in range(strip):
            put_row(ds, h + 1, [dpre[h, pl.ds(f * width, width)] for f in range(nf)])
        for h in range(strip):
            total = conv(ds, h + 2, wb, 0) + conv(ds, h + 1, wb, 1) + conv(ds, h, wb, 2)
            for f in range(nf):
                gi_ref[f, h] = total[f * width : (f + 1) * width]

    start_core(0)
    spatial_terms(1, 1, 0)
    spatial_terms(2, 1, 1)
    start_core(1)
    start_rows(0)
    start_rows(1)
    mixed()
    start_z(0)
    image_gradient()
    start_z(1)
    start_around(0)
    start_around(1)
    start_back(0)
    start_back(1)
    finish(0)
    finish(1)

    for copy in sent:
        copy.wait_send()
    for copy, there in (
        (x_up, has_up), (x_down, has_down), (c_prev, has_prev),
        (a_next, has_next), (d_up, has_up), (d_down, has_down),
    ):
        pl.when(there)(copy.wait_send)


def per_device(nfd, nrd, images, spatial_weight, temporal_weight, cotangent):
    nf, strip, width, chans = images.shape
    wide, three = nf * width, 3 * chans
    nz, share = nfd // 2, chans // nrd
    piece = -(-(3 * share) // nz)
    piece = -(-piece // 8) * 8
    factor = 1.0 / math.sqrt(nf * nfd * strip * nrd * width)
    n_sems = 6 + GROUPS * (2 + (nrd - 1) + 2 * (nz - 1))
    vmem = pl.BlockSpec(memory_space=pltpu.VMEM)
    mixed, gradient, grads = pl.pallas_call(
        functools.partial(kernel, nfd, nrd, share, piece, factor),
        out_shape=(
            jax.ShapeDtypeStruct(images.shape, F32),
            jax.ShapeDtypeStruct(images.shape, F32),
            jax.ShapeDtypeStruct((GROUPS, 2, nz * piece, chans), F32),
        ),
        in_specs=[vmem] * 4,
        out_specs=(vmem,) * 3,
        scratch_shapes=[
            pltpu.VMEM((strip + 2, wide, 2 * three), BF16),
            pltpu.VMEM((strip + 2, wide, 2 * three), BF16),
            pltpu.VMEM((3, three, 2 * chans), BF16),
            pltpu.VMEM((3, three, 2 * chans), BF16),
            pltpu.VMEM((3, chans, 2 * chans), BF16),
            pltpu.VMEM((3, chans, 2 * chans), BF16),
            pltpu.VMEM((2, nf, width, chans), F32),
            pltpu.VMEM((nf, strip, width, chans), F32),
            pltpu.VMEM((strip, wide, chans), F32),
            pltpu.VMEM((2, wide, chans), F32),
            pltpu.VMEM((strip, wide, chans), F32),
            pltpu.VMEM((strip, wide, chans), F32),
            pltpu.VMEM((2, strip, 2 * wide, chans), BF16),
            pltpu.VMEM((2, strip, 2 * wide, chans), BF16),
            pltpu.VMEM((GROUPS, 2, 3, chans, chans), F32),
            pltpu.VMEM((GROUPS, 3, chans, chans), F32),
            pltpu.VMEM((GROUPS, 3, chans, chans), F32),
            pltpu.VMEM((GROUPS, nrd - 1, 3, share, chans), F32),
            pltpu.VMEM((GROUPS, nz * piece, chans), F32),
            pltpu.VMEM((GROUPS, nz - 1, piece, chans), F32),
            pltpu.VMEM((GROUPS, 1, piece, chans), F32),
            pltpu.VMEM((GROUPS, 2, nz * piece, chans), F32),
            pltpu.SemaphoreType.DMA((n_sems,)),
            pltpu.SemaphoreType.DMA((n_sems,)),
        ],
        compiler_params=pltpu.CompilerParams(
            collective_id=0, has_side_effects=True, vmem_limit_bytes=24 * 2**20
        ),
        cost_estimate=pl.CostEstimate(flops=1_400_000_000, bytes_accessed=2_000_000, transcendentals=50_000),
    )(images, spatial_weight, temporal_weight, cotangent)
    grads = grads[:, :, : 3 * share].reshape(GROUPS * 2, 3, share, chans).transpose(0, 1, 3, 2)
    return images + mixed, cotangent + gradient, grads[1:], grads[0]


def solution(mesh):
    return jax.shard_map(
        functools.partial(per_device, mesh.shape["frames"], mesh.shape["rows"]),
        mesh=mesh,
        in_specs=(P("frames", "rows", None, None), P(), P(), P("frames", "rows", None, None)),
        out_specs=(
            P("frames", "rows", None, None),
            P("frames", "rows", None, None),
            P(None, None, None, "rows"),
            P(None, None, "rows"),
        ),
        check_vma=False,
    )
```

```python
import functools
import math

import jax
import jax.numpy as jnp
from jax import lax
from jax.experimental import pallas as pl
from jax.experimental.pallas import tpu as pltpu
from jax.sharding import PartitionSpec as P

MESH = pl.DeviceIdType.MESH
F32, BF16 = jnp.float32, jnp.bfloat16
GROUPS = 2
VMEM_LIMIT = 60 * 2**20


def split(value):
    high = value.astype(BF16)
    return high, (value - high.astype(F32)).astype(BF16)


def dot(a, b):
    return jnp.dot(a, b, preferred_element_type=F32)


def put_weight(dst, index, value):
    high, low = split(value)
    n = value.shape[1]
    dst[index, :, :n] = high
    dst[index, :, n:] = low


def product(high, low, both):
    n = both.shape[1] // 2
    wide = dot(high, both)
    return wide[:, :n] + wide[:, n:] + dot(low, both[:, :n])


def put_row(dst, row, frames):
    width, chans = frames[0].shape
    at = lax.broadcasted_iota(jnp.int32, (width, chans), 0)
    for f, value in enumerate(frames):
        before = jnp.where(at == 0, 0.0, pltpu.roll(value, 1, 0))
        after = jnp.where(at == width - 1, 0.0, pltpu.roll(value, width - 1, 0))
        rows = pl.ds(f * width, width)
        for b, moved in enumerate((before, value, after)):
            high, low = split(moved)
            dst[row, rows, b * chans : (b + 1) * chans] = high
            dst[row, rows, (3 + b) * chans : (4 + b) * chans] = low


def kernel(
    nfd, nrd, share, piece, factor,
    x_hbm, sw_hbm, tw_hbm, cot_hbm, mix_hbm, gi_hbm, gr_hbm,
    x_ref, sw_ref, tw_ref, cot_ref, mix_ref, gi_ref, load_sem, store_sem, xs, ds, wf, wb, tf, tb, xhalo, chalo, ahalo, dhalo, act, dpre, cots, acts,
    terms, core_in, half, rows_in, plane, z_in, own, final, send_sem, recv_sem,
):
    nf, strip, width, chans = x_ref.shape
    assert nf == 2 and strip == 2
    wide = nf * width
    three = 3 * chans
    fr, ro = lax.axis_index("frames"), lax.axis_index("rows")
    core, z = lax.rem(fr, 2), lax.div(fr, 2)
    nz = nfd // 2
    other = fr + 1 - 2 * core
    n_sems = [0]
    sent, stores = [], []

    def remote(src, dst, **where):
        n = n_sems[0]
        n_sems[0] += 1
        return pltpu.make_async_remote_copy(
            src_ref=src, dst_ref=dst, send_sem=send_sem.at[n], recv_sem=recv_sem.at[n],
            device_id=where, device_id_type=MESH,
        )

    def send(src, dst, **where):
        copy = remote(src, dst, **where)
        copy.start()
        sent.append(copy)
        return copy

    loads = [
        pltpu.make_async_copy(src, dst, load_sem.at[n])
        for n, (src, dst) in enumerate(
            ((x_hbm, x_ref), (cot_hbm, cot_ref), (tw_hbm, tw_ref), (sw_hbm, sw_ref))
        )
    ]
    for load in loads:
        load.start()
    barrier = pltpu.get_barrier_semaphore()
    for o in range(1, nrd):
        pl.semaphore_signal(barrier, inc=1, device_id={"rows": lax.rem(ro + o, nrd)}, device_id_type=MESH)
    for o in range(1, nfd):
        pl.semaphore_signal(barrier, inc=1, device_id={"frames": lax.rem(fr + o, nfd)}, device_id_type=MESH)

    loads[0].wait()
    for h in range(strip):
        put_row(xs, h + 1, [x_ref[f, h] for f in range(nf)])
    loads[1].wait()

    pl.semaphore_wait(barrier, nrd - 1 + nfd - 1)

    has_up, has_down = ro > 0, ro < nrd - 1
    has_prev, has_next = fr > 0, fr < nfd - 1
    up, down = lax.rem(ro + nrd - 1, nrd), lax.rem(ro + 1, nrd)
    prev, following = lax.rem(fr + nfd - 1, nfd), lax.rem(fr + 1, nfd)
    x_up = remote(x_ref.at[:, 0], xhalo.at[1], rows=up)
    x_down = remote(x_ref.at[:, strip - 1], xhalo.at[0], rows=down)
    c_prev = remote(cot_ref, chalo, frames=prev)
    a_next = remote(act, ahalo, frames=following)
    d_up = remote(dpre.at[0], dhalo.at[1], rows=up)
    d_down = remote(dpre.at[strip - 1], dhalo.at[0], rows=down)

    def receive(copy, there, zeroed):
        @pl.when(there)
        def _():
            copy.wait_recv()

        @pl.when(jnp.logical_not(there))
        def _():
            zeroed[...] = jnp.zeros(zeroed.shape, F32)

    @pl.when(has_up)
    def _():
        x_up.start()

    @pl.when(has_down)
    def _():
        x_down.start()

    @pl.when(has_prev)
    def _():
        c_prev.start()

    def put_cots(first, src):
        for f in range(nf):
            for h in range(strip):
                rows = pl.ds(first + f * width, width)
                high, low = split(src[f, h])
                cots[0, h, rows, :] = high
                cots[1, h, rows, :] = low

    put_cots(0, cot_ref)
    loads[2].wait()
    for k in range(3):
        put_weight(tb, k, tw_ref[k].T)
        put_weight(tf, k, tw_ref[k])
    loads[3].wait()
    for i in range(3):
        put_weight(wf, i, sw_ref[i].reshape(three, chans))

    def conv(src, row, count, weight, i):
        rows = src[row : row + count].reshape(count * wide, 2 * three)
        return product(rows[:, :three], rows[:, three:], weight[i])

    middle = conv(xs, 1, 2, wf, 1)
    pre = [middle[:wide] + conv(xs, 2, 1, wf, 2), middle[wide:] + conv(xs, 1, 1, wf, 0)]
    for i in range(3):
        put_weight(wb, i, jnp.concatenate([sw_ref[i, 2 - b].T for b in range(3)], axis=0))

    def temporal(src, shift, weight, k):
        rows = pl.ds(shift * width, wide)
        both = [src[p, :, rows, :].reshape(strip * wide, chans) for p in range(2)]
        return product(both[0], both[1], weight[k])

    dact = temporal(cots, 0, tb, 0)
    receive(c_prev, has_next, chalo)
    put_cots(wide, chalo)
    dact = dact + temporal(cots, 1, tb, 1) + temporal(cots, 2, tb, 2)

    receive(x_down, has_up, xhalo.at[0])
    put_row(xs, 0, [xhalo[0, f] for f in range(nf)])
    receive(x_up, has_down, xhalo.at[1])
    put_row(xs, 3, [xhalo[1, f] for f in range(nf)])
    pre = [pre[0] + conv(xs, 0, 1, wf, 0), pre[1] + conv(xs, 3, 1, wf, 2)]

    both_act, both_dpre = [], []
    for h in range(strip):
        sig = 1.0 / (1.0 + jnp.exp(-pre[h]))
        act_h = pre[h] * sig
        act[h] = act_h
        dpre_h = dact[h * wide : (h + 1) * wide] * sig * (1.0 + pre[h] * (1.0 - sig))
        dpre[h] = dpre_h
        both_act.append(act_h)
        both_dpre.append(dpre_h)

    @pl.when(has_next)
    def _():
        a_next.start()

    act_t = split(jnp.concatenate(both_act, axis=0).T)
    for k in range(3):
        rows = pl.ds(k * width, wide)
        c_high = cots[0, :, rows, :].reshape(strip * wide, chans)
        c_low = cots[1, :, rows, :].reshape(strip * wide, chans)
        term = dot(act_t[0], c_high) + dot(act_t[0], c_low) + dot(act_t[1], c_high)
        terms[0, 0, k] = term.T
    dpre_t = split(jnp.concatenate(both_dpre, axis=0).T)

    def spatial_terms(i, g, side):
        src = xs[i : i + strip].reshape(strip * wide, 2 * three)
        wide_term = dot(dpre_t[0], src)
        term = wide_term[:, :three] + wide_term[:, three:] + dot(dpre_t[1], src[:, :three])
        for j in range(3):
            terms[g, side, j] = term[:, j * chans : (j + 1) * chans]

    spatial_terms(1, 0, 1)
    to_core = [None] * GROUPS
    to_rows = [None] * GROUPS
    to_z = [None] * GROUPS
    around_z = [None] * GROUPS
    back = [None] * GROUPS

    def start_core(g):
        to_core[g] = send(terms.at[g, 1 - core], core_in.at[g], frames=other)

    def start_rows(g):
        to_core[g].wait_recv()
        half[g] = terms[g, core] + core_in[g]
        to_rows[g] = []
        for o in range(1, nrd):
            target = lax.rem(ro + o, nrd)
            part = pl.ds(pl.multiple_of(target * share, 8), share)
            to_rows[g].append(send(half.at[g, :, part, :], rows_in.at[g, o - 1], rows=target))

    def start_z(g):
        total = half[g, :, pl.ds(pl.multiple_of(ro * share, 8), share), :]
        for o in range(1, nrd):
            to_rows[g][o - 1].wait_recv()
            total = total + rows_in[g, o - 1]
        plane[g, : 3 * share] = total.reshape(3 * share, chans) * factor
        if nz * piece > 3 * share:
            plane[g, 3 * share :] = jnp.zeros((nz * piece - 3 * share, chans), F32)
        to_z[g] = []
        for o in range(1, nz):
            target = lax.rem(z + o, nz)
            part = pl.ds(pl.multiple_of(target * piece, 8), piece)
            to_z[g].append(send(plane.at[g, part], z_in.at[g, o - 1], frames=2 * target + core))

    def start_around(g):
        mine = pl.ds(pl.multiple_of(z * piece, 8), piece)
        total = plane[g, mine]
        for o in range(1, nz):
            to_z[g][o - 1].wait_recv()
            total = total + z_in[g, o - 1]
        own[g, 0] = total
        final[g, core, mine] = total
        around_z[g] = []
        for o in range(1, nz):
            target = lax.rem(z + o, nz)
            around_z[g].append(send(own.at[g, 0], final.at[g, core, mine], frames=2 * target + core))

    def start_back(g):
        for copy in around_z[g]:
            copy.wait_recv()
        back[g] = send(final.at[g, core], final.at[g, core], frames=other)

    def finish(g):
        back[g].wait_recv()
        stores.append(pltpu.make_async_copy(final.at[g], gr_hbm.at[g], store_sem.at[2 + g]))
        stores[-1].start()

    def put_acts(first, src):
        for h in range(strip):
            high, low = split(src[h])
            acts[0, h, pl.ds(first, wide), :] = high
            acts[1, h, pl.ds(first, wide), :] = low

    start_core(0)
    spatial_terms(0, 1, 0)
    spatial_terms(2, 1, 1)
    start_core(1)
    start_rows(0)
    for h in range(strip):
        put_row(ds, h + 1, [dpre[h, pl.ds(f * width, width)] for f in range(nf)])
    start_rows(1)

    @pl.when(has_up)
    def _():
        d_up.start()

    @pl.when(has_down)
    def _():
        d_down.start()

    put_acts(wide, act)
    mixed = temporal(acts, 2, tf, 0)
    receive(a_next, has_prev, ahalo)
    put_acts(0, ahalo)
    mixed = mixed + temporal(acts, 1, tf, 1) + temporal(acts, 0, tf, 2)
    for h in range(strip):
        for f in range(nf):
            at = h * wide + f * width
            mix_ref[f, h] = x_ref[f, h] + mixed[at : at + width]
    stores.append(pltpu.make_async_copy(mix_ref, mix_hbm, store_sem.at[0]))
    stores[-1].start()
    start_z(0)

    middle = conv(ds, 1, 2, wb, 1)
    grad = [middle[:wide] + conv(ds, 2, 1, wb, 0), middle[wide:] + conv(ds, 1, 1, wb, 2)]
    start_z(1)
    start_around(0)
    receive(d_down, has_up, dhalo.at[0])
    put_row(ds, 0, [dhalo[0, pl.ds(f * width, width)] for f in range(nf)])
    receive(d_up, has_down, dhalo.at[1])
    put_row(ds, 3, [dhalo[1, pl.ds(f * width, width)] for f in range(nf)])
    grad = [grad[0] + conv(ds, 0, 1, wb, 2), grad[1] + conv(ds, 3, 1, wb, 0)]
    for h in range(strip):
        for f in range(nf):
            at = f * width
            gi_ref[f, h] = cot_ref[f, h] + grad[h][at : at + width]
    stores.append(pltpu.make_async_copy(gi_ref, gi_hbm, store_sem.at[1]))
    stores[-1].start()
    start_around(1)
    start_back(0)
    start_back(1)
    finish(0)
    finish(1)

    for copy in stores:
        copy.wait()
    for copy in sent:
        copy.wait_send()
    for copy, there in (
        (x_up, has_up), (x_down, has_down), (c_prev, has_prev),
        (a_next, has_next), (d_up, has_up), (d_down, has_down),
    ):
        pl.when(there)(copy.wait_send)


def write(rows, mix_ref, gi_ref, gr_ref, out_ref, grad_ref, spatial_ref, temporal_ref, sem):
    pairs = [(mix_ref, out_ref), (gi_ref, grad_ref), (gr_ref.at[0, 0, pl.ds(0, rows)], temporal_ref)]
    for i, (g, side) in enumerate(((1, 0), (0, 1), (1, 1))):
        pairs.append((gr_ref.at[g, side, pl.ds(0, rows)], spatial_ref.at[i]))
    copies = [pltpu.make_async_copy(src, dst, sem.at[n]) for n, (src, dst) in enumerate(pairs)]
    for copy in copies:
        copy.start()
    for copy in copies:
        copy.wait()


def per_device(nfd, nrd, images, spatial_weight, temporal_weight, cotangent):
    nf, strip, width, chans = images.shape
    wide, three = nf * width, 3 * chans
    nz, share = nfd // 2, chans // nrd
    piece = -(-(3 * share) // nz)
    piece = -(-piece // 8) * 8
    factor = 1.0 / math.sqrt(nf * nfd * strip * nrd * width)
    n_sems = 6 + GROUPS * (2 + (nrd - 1) + 2 * (nz - 1))
    hbm = pl.BlockSpec(memory_space=pltpu.HBM)
    operands = (images, spatial_weight, temporal_weight, cotangent)
    results = pl.pallas_call(
        functools.partial(kernel, nfd, nrd, share, piece, factor),
        out_shape=(
            jax.ShapeDtypeStruct(images.shape, F32),
            jax.ShapeDtypeStruct(images.shape, F32),
            jax.ShapeDtypeStruct((GROUPS, 2, nz * piece, chans), F32),
        ),
        in_specs=[hbm] * 4,
        out_specs=(hbm,) * 3,
        scratch_shapes=[
            *(pltpu.VMEM(a.shape, F32) for a in operands),
            pltpu.VMEM(images.shape, F32),
            pltpu.VMEM(images.shape, F32),
            pltpu.SemaphoreType.DMA((4,)),
            pltpu.SemaphoreType.DMA((2 + GROUPS,)),
            pltpu.VMEM((strip + 2, wide, 2 * three), BF16),
            pltpu.VMEM((strip + 2, wide, 2 * three), BF16),
            pltpu.VMEM((3, three, 2 * chans), BF16),
            pltpu.VMEM((3, three, 2 * chans), BF16),
            pltpu.VMEM((3, chans, 2 * chans), BF16),
            pltpu.VMEM((3, chans, 2 * chans), BF16),
            pltpu.VMEM((2, nf, width, chans), F32),
            pltpu.VMEM((nf, strip, width, chans), F32),
            pltpu.VMEM((strip, wide, chans), F32),
            pltpu.VMEM((2, wide, chans), F32),
            pltpu.VMEM((strip, wide, chans), F32),
            pltpu.VMEM((strip, wide, chans), F32),
            pltpu.VMEM((2, strip, 2 * wide, chans), BF16),
            pltpu.VMEM((2, strip, 2 * wide, chans), BF16),
            pltpu.VMEM((GROUPS, 2, 3, chans, chans), F32),
            pltpu.VMEM((GROUPS, 3, chans, chans), F32),
            pltpu.VMEM((GROUPS, 3, chans, chans), F32),
            pltpu.VMEM((GROUPS, nrd - 1, 3, share, chans), F32),
            pltpu.VMEM((GROUPS, nz * piece, chans), F32),
            pltpu.VMEM((GROUPS, nz - 1, piece, chans), F32),
            pltpu.VMEM((GROUPS, 1, piece, chans), F32),
            pltpu.VMEM((GROUPS, 2, nz * piece, chans), F32),
            pltpu.SemaphoreType.DMA((n_sems,)),
            pltpu.SemaphoreType.DMA((n_sems,)),
        ],
        compiler_params=pltpu.CompilerParams(
            collective_id=0, has_side_effects=True, vmem_limit_bytes=VMEM_LIMIT
        ),
        cost_estimate=pl.CostEstimate(flops=1_400_000_000, bytes_accessed=2_000_000, transcendentals=50_000),
    )(*operands)
    out, gradient, spatial, temporal = pl.pallas_call(
        functools.partial(write, 3 * share),
        out_shape=(
            jax.ShapeDtypeStruct(images.shape, F32),
            jax.ShapeDtypeStruct(images.shape, F32),
            jax.ShapeDtypeStruct((3, 3 * share, chans), F32),
            jax.ShapeDtypeStruct((3 * share, chans), F32),
        ),
        in_specs=[hbm] * 3,
        out_specs=(hbm,) * 4,
        scratch_shapes=[pltpu.SemaphoreType.DMA((6,))],
        compiler_params=pltpu.CompilerParams(vmem_limit_bytes=VMEM_LIMIT),
        cost_estimate=pl.CostEstimate(flops=0, bytes_accessed=1_200_000, transcendentals=0),
    )(*results)
    return (
        out,
        gradient,
        spatial.reshape(3, 3, share, chans).transpose(0, 1, 3, 2),
        temporal.reshape(3, share, chans).transpose(0, 2, 1),
    )


def solution(mesh):
    return jax.shard_map(
        functools.partial(per_device, mesh.shape["frames"], mesh.shape["rows"]),
        mesh=mesh,
        in_specs=(P("frames", "rows", None, None), P(), P(), P("frames", "rows", None, None)),
        out_specs=(
            P("frames", "rows", None, None),
            P("frames", "rows", None, None),
            P(None, None, None, "rows"),
            P(None, None, "rows"),
        ),
        check_vma=False,
    )
```

```python
import functools
import math

import jax
import jax.numpy as jnp
from jax import lax
from jax.experimental import pallas as pl
from jax.experimental.pallas import tpu as pltpu
from jax.sharding import PartitionSpec as P

MESH = pl.DeviceIdType.MESH
F32, BF16 = jnp.float32, jnp.bfloat16
GROUPS = 2
VMEM_LIMIT = 24 * 2**20


def split(value):
    high = value.astype(BF16)
    return high, (value - high.astype(F32)).astype(BF16)


def dot(a, b):
    return jnp.dot(a, b, preferred_element_type=F32)


def put_weight(dst, index, value):
    high, low = split(value)
    n = value.shape[1]
    dst[index, :, :n] = high
    dst[index, :, n:] = low


def product(high, low, both):
    n = both.shape[1] // 2
    wide = dot(high, both)
    return wide[:, :n] + wide[:, n:] + dot(low, both[:, :n])


def put_row(dst, row, frames):
    width, chans = frames[0].shape
    at = lax.broadcasted_iota(jnp.int32, (width, chans), 0)
    for f, value in enumerate(frames):
        before = jnp.where(at == 0, 0.0, pltpu.roll(value, 1, 0))
        after = jnp.where(at == width - 1, 0.0, pltpu.roll(value, width - 1, 0))
        rows = pl.ds(f * width, width)
        for b, moved in enumerate((before, value, after)):
            high, low = split(moved)
            dst[row, rows, b * chans : (b + 1) * chans] = high
            dst[row, rows, (3 + b) * chans : (4 + b) * chans] = low


def kernel(
    nfd, nrd, share, piece, factor,
    x_hbm, sw_hbm, tw_hbm, cot_hbm, mix_ref, gi_ref, gr_ref,
    x_ref, sw_ref, tw_ref, cot_ref, load_sem, xs, ds, wf, wb, tf, tb, xhalo, chalo, ahalo, dhalo, act, dpre, cots, acts,
    terms, core_in, half, rows_in, plane, z_in, own, final, send_sem, recv_sem,
):
    nf, strip, width, chans = x_ref.shape
    assert nf == 2 and strip == 2
    wide = nf * width
    three = 3 * chans
    fr, ro = lax.axis_index("frames"), lax.axis_index("rows")
    core, z = lax.rem(fr, 2), lax.div(fr, 2)
    nz = nfd // 2
    other = fr + 1 - 2 * core
    n_sems = [0]
    sent = []

    def remote(src, dst, **where):
        n = n_sems[0]
        n_sems[0] += 1
        return pltpu.make_async_remote_copy(
            src_ref=src, dst_ref=dst, send_sem=send_sem.at[n], recv_sem=recv_sem.at[n],
            device_id=where, device_id_type=MESH,
        )

    def send(src, dst, **where):
        copy = remote(src, dst, **where)
        copy.start()
        sent.append(copy)
        return copy

    loads = [
        pltpu.make_async_copy(src, dst, load_sem.at[n])
        for n, (src, dst) in enumerate(
            ((x_hbm, x_ref), (cot_hbm, cot_ref), (tw_hbm, tw_ref), (sw_hbm, sw_ref))
        )
    ]
    for load in loads:
        load.start()
    barrier = pltpu.get_barrier_semaphore()
    for o in range(1, nrd):
        pl.semaphore_signal(barrier, inc=1, device_id={"rows": lax.rem(ro + o, nrd)}, device_id_type=MESH)
    for o in range(1, nfd):
        pl.semaphore_signal(barrier, inc=1, device_id={"frames": lax.rem(fr + o, nfd)}, device_id_type=MESH)

    loads[0].wait()
    for h in range(strip):
        put_row(xs, h + 1, [x_ref[f, h] for f in range(nf)])
    loads[1].wait()

    pl.semaphore_wait(barrier, nrd - 1 + nfd - 1)

    has_up, has_down = ro > 0, ro < nrd - 1
    has_prev, has_next = fr > 0, fr < nfd - 1
    up, down = lax.rem(ro + nrd - 1, nrd), lax.rem(ro + 1, nrd)
    prev, following = lax.rem(fr + nfd - 1, nfd), lax.rem(fr + 1, nfd)
    x_up = remote(x_ref.at[:, 0], xhalo.at[1], rows=up)
    x_down = remote(x_ref.at[:, strip - 1], xhalo.at[0], rows=down)
    c_prev = remote(cot_ref, chalo, frames=prev)
    a_next = remote(act, ahalo, frames=following)
    d_up = remote(dpre.at[0], dhalo.at[1], rows=up)
    d_down = remote(dpre.at[strip - 1], dhalo.at[0], rows=down)

    def receive(copy, there, zeroed):
        @pl.when(there)
        def _():
            copy.wait_recv()

        @pl.when(jnp.logical_not(there))
        def _():
            zeroed[...] = jnp.zeros(zeroed.shape, F32)

    @pl.when(has_up)
    def _():
        x_up.start()

    @pl.when(has_down)
    def _():
        x_down.start()

    @pl.when(has_prev)
    def _():
        c_prev.start()

    def put_cots(first, src):
        for f in range(nf):
            for h in range(strip):
                rows = pl.ds(first + f * width, width)
                high, low = split(src[f, h])
                cots[0, h, rows, :] = high
                cots[1, h, rows, :] = low

    put_cots(0, cot_ref)
    loads[2].wait()
    for k in range(3):
        put_weight(tb, k, tw_ref[k].T)
        put_weight(tf, k, tw_ref[k])
    loads[3].wait()
    for i in range(3):
        put_weight(wf, i, sw_ref[i].reshape(three, chans))

    def conv(src, row, count, weight, i):
        rows = src[row : row + count].reshape(count * wide, 2 * three)
        return product(rows[:, :three], rows[:, three:], weight[i])

    middle = conv(xs, 1, 2, wf, 1)
    pre = [middle[:wide] + conv(xs, 2, 1, wf, 2), middle[wide:] + conv(xs, 1, 1, wf, 0)]
    for i in range(3):
        put_weight(wb, i, jnp.concatenate([sw_ref[i, 2 - b].T for b in range(3)], axis=0))

    def temporal(src, shift, weight, k):
        rows = pl.ds(shift * width, wide)
        both = [src[p, :, rows, :].reshape(strip * wide, chans) for p in range(2)]
        return product(both[0], both[1], weight[k])

    dact = temporal(cots, 0, tb, 0)
    receive(c_prev, has_next, chalo)
    put_cots(wide, chalo)
    dact = dact + temporal(cots, 1, tb, 1) + temporal(cots, 2, tb, 2)

    receive(x_down, has_up, xhalo.at[0])
    put_row(xs, 0, [xhalo[0, f] for f in range(nf)])
    receive(x_up, has_down, xhalo.at[1])
    put_row(xs, 3, [xhalo[1, f] for f in range(nf)])
    pre = [pre[0] + conv(xs, 0, 1, wf, 0), pre[1] + conv(xs, 3, 1, wf, 2)]

    both_act, both_dpre = [], []
    for h in range(strip):
        sig = 1.0 / (1.0 + jnp.exp(-pre[h]))
        act_h = pre[h] * sig
        act[h] = act_h
        dpre_h = dact[h * wide : (h + 1) * wide] * sig * (1.0 + pre[h] * (1.0 - sig))
        dpre[h] = dpre_h
        both_act.append(act_h)
        both_dpre.append(dpre_h)

    @pl.when(has_next)
    def _():
        a_next.start()

    act_t = split(jnp.concatenate(both_act, axis=0).T)
    for k in range(3):
        rows = pl.ds(k * width, wide)
        c_high = cots[0, :, rows, :].reshape(strip * wide, chans)
        c_low = cots[1, :, rows, :].reshape(strip * wide, chans)
        term = dot(act_t[0], c_high) + dot(act_t[0], c_low) + dot(act_t[1], c_high)
        terms[0, 0, k] = term.T
    dpre_t = split(jnp.concatenate(both_dpre, axis=0).T)

    def spatial_terms(i, g, side):
        src = xs[i : i + strip].reshape(strip * wide, 2 * three)
        wide_term = dot(dpre_t[0], src)
        term = wide_term[:, :three] + wide_term[:, three:] + dot(dpre_t[1], src[:, :three])
        for j in range(3):
            terms[g, side, j] = term[:, j * chans : (j + 1) * chans]

    spatial_terms(1, 0, 1)
    to_core = [None] * GROUPS
    to_rows = [None] * GROUPS
    to_z = [None] * GROUPS
    around_z = [None] * GROUPS
    back = [None] * GROUPS

    def start_core(g):
        to_core[g] = send(terms.at[g, 1 - core], core_in.at[g], frames=other)

    def start_rows(g):
        to_core[g].wait_recv()
        half[g] = terms[g, core] + core_in[g]
        to_rows[g] = []
        for o in range(1, nrd):
            target = lax.rem(ro + o, nrd)
            part = pl.ds(pl.multiple_of(target * share, 8), share)
            to_rows[g].append(send(half.at[g, :, part, :], rows_in.at[g, o - 1], rows=target))

    def start_z(g):
        total = half[g, :, pl.ds(pl.multiple_of(ro * share, 8), share), :]
        for o in range(1, nrd):
            to_rows[g][o - 1].wait_recv()
            total = total + rows_in[g, o - 1]
        plane[g, : 3 * share] = total.reshape(3 * share, chans) * factor
        if nz * piece > 3 * share:
            plane[g, 3 * share :] = jnp.zeros((nz * piece - 3 * share, chans), F32)
        to_z[g] = []
        for o in range(1, nz):
            target = lax.rem(z + o, nz)
            part = pl.ds(pl.multiple_of(target * piece, 8), piece)
            to_z[g].append(send(plane.at[g, part], z_in.at[g, o - 1], frames=2 * target + core))

    def start_around(g):
        mine = pl.ds(pl.multiple_of(z * piece, 8), piece)
        total = plane[g, mine]
        for o in range(1, nz):
            to_z[g][o - 1].wait_recv()
            total = total + z_in[g, o - 1]
        own[g, 0] = total
        final[g, core, mine] = total
        around_z[g] = []
        for o in range(1, nz):
            target = lax.rem(z + o, nz)
            around_z[g].append(send(own.at[g, 0], final.at[g, core, mine], frames=2 * target + core))

    def start_back(g):
        for copy in around_z[g]:
            copy.wait_recv()
        back[g] = send(final.at[g, core], final.at[g, core], frames=other)

    def finish(g):
        back[g].wait_recv()
        gr_ref[g] = final[g]

    def put_acts(first, src):
        for h in range(strip):
            high, low = split(src[h])
            acts[0, h, pl.ds(first, wide), :] = high
            acts[1, h, pl.ds(first, wide), :] = low

    start_core(0)
    spatial_terms(0, 1, 0)
    spatial_terms(2, 1, 1)
    start_core(1)
    start_rows(0)
    for h in range(strip):
        put_row(ds, h + 1, [dpre[h, pl.ds(f * width, width)] for f in range(nf)])
    start_rows(1)

    @pl.when(has_up)
    def _():
        d_up.start()

    @pl.when(has_down)
    def _():
        d_down.start()

    put_acts(wide, act)
    mixed = temporal(acts, 2, tf, 0)
    receive(a_next, has_prev, ahalo)
    put_acts(0, ahalo)
    mixed = mixed + temporal(acts, 1, tf, 1) + temporal(acts, 0, tf, 2)
    for h in range(strip):
        for f in range(nf):
            at = h * wide + f * width
            mix_ref[f, h] = x_ref[f, h] + mixed[at : at + width]
    start_z(0)

    middle = conv(ds, 1, 2, wb, 1)
    grad = [middle[:wide] + conv(ds, 2, 1, wb, 0), middle[wide:] + conv(ds, 1, 1, wb, 2)]
    start_z(1)
    start_around(0)
    receive(d_down, has_up, dhalo.at[0])
    put_row(ds, 0, [dhalo[0, pl.ds(f * width, width)] for f in range(nf)])
    receive(d_up, has_down, dhalo.at[1])
    put_row(ds, 3, [dhalo[1, pl.ds(f * width, width)] for f in range(nf)])
    grad = [grad[0] + conv(ds, 0, 1, wb, 2), grad[1] + conv(ds, 3, 1, wb, 0)]
    for h in range(strip):
        for f in range(nf):
            at = f * width
            gi_ref[f, h] = cot_ref[f, h] + grad[h][at : at + width]
    start_around(1)
    start_back(0)
    start_back(1)
    finish(0)
    finish(1)

    for copy in sent:
        copy.wait_send()
    for copy, there in (
        (x_up, has_up), (x_down, has_down), (c_prev, has_prev),
        (a_next, has_next), (d_up, has_up), (d_down, has_down),
    ):
        pl.when(there)(copy.wait_send)


def write(rows, mix_ref, gi_ref, gr_ref, out_ref, grad_ref, spatial_ref, temporal_ref, sem):
    pairs = [(mix_ref, out_ref), (gi_ref, grad_ref), (gr_ref.at[0, 0, pl.ds(0, rows)], temporal_ref)]
    for i, (g, side) in enumerate(((1, 0), (0, 1), (1, 1))):
        pairs.append((gr_ref.at[g, side, pl.ds(0, rows)], spatial_ref.at[i]))
    copies = [pltpu.make_async_copy(src, dst, sem.at[n]) for n, (src, dst) in enumerate(pairs)]
    for copy in copies:
        copy.start()
    for copy in copies:
        copy.wait()


def per_device(nfd, nrd, images, spatial_weight, temporal_weight, cotangent):
    nf, strip, width, chans = images.shape
    wide, three = nf * width, 3 * chans
    nz, share = nfd // 2, chans // nrd
    piece = -(-(3 * share) // nz)
    piece = -(-piece // 8) * 8
    factor = 1.0 / math.sqrt(nf * nfd * strip * nrd * width)
    n_sems = 6 + GROUPS * (2 + (nrd - 1) + 2 * (nz - 1))
    vmem, hbm = (pl.BlockSpec(memory_space=space) for space in (pltpu.VMEM, pltpu.HBM))
    operands = (images, spatial_weight, temporal_weight, cotangent)
    operands = [pltpu.with_memory_space_constraint(a, pltpu.HBM) for a in operands]
    results = pl.pallas_call(
        functools.partial(kernel, nfd, nrd, share, piece, factor),
        out_shape=(
            pltpu.VMEM(images.shape, F32),
            pltpu.VMEM(images.shape, F32),
            pltpu.VMEM((GROUPS, 2, nz * piece, chans), F32),
        ),
        in_specs=[hbm] * 4,
        out_specs=(vmem,) * 3,
        scratch_shapes=[
            *(pltpu.VMEM(a.shape, F32) for a in operands),
            pltpu.SemaphoreType.DMA((4,)),
            pltpu.VMEM((strip + 2, wide, 2 * three), BF16),
            pltpu.VMEM((strip + 2, wide, 2 * three), BF16),
            pltpu.VMEM((3, three, 2 * chans), BF16),
            pltpu.VMEM((3, three, 2 * chans), BF16),
            pltpu.VMEM((3, chans, 2 * chans), BF16),
            pltpu.VMEM((3, chans, 2 * chans), BF16),
            pltpu.VMEM((2, nf, width, chans), F32),
            pltpu.VMEM((nf, strip, width, chans), F32),
            pltpu.VMEM((strip, wide, chans), F32),
            pltpu.VMEM((2, wide, chans), F32),
            pltpu.VMEM((strip, wide, chans), F32),
            pltpu.VMEM((strip, wide, chans), F32),
            pltpu.VMEM((2, strip, 2 * wide, chans), BF16),
            pltpu.VMEM((2, strip, 2 * wide, chans), BF16),
            pltpu.VMEM((GROUPS, 2, 3, chans, chans), F32),
            pltpu.VMEM((GROUPS, 3, chans, chans), F32),
            pltpu.VMEM((GROUPS, 3, chans, chans), F32),
            pltpu.VMEM((GROUPS, nrd - 1, 3, share, chans), F32),
            pltpu.VMEM((GROUPS, nz * piece, chans), F32),
            pltpu.VMEM((GROUPS, nz - 1, piece, chans), F32),
            pltpu.VMEM((GROUPS, 1, piece, chans), F32),
            pltpu.VMEM((GROUPS, 2, nz * piece, chans), F32),
            pltpu.SemaphoreType.DMA((n_sems,)),
            pltpu.SemaphoreType.DMA((n_sems,)),
        ],
        compiler_params=pltpu.CompilerParams(
            collective_id=0, has_side_effects=True, vmem_limit_bytes=VMEM_LIMIT
        ),
        cost_estimate=pl.CostEstimate(flops=1_400_000_000, bytes_accessed=2_000_000, transcendentals=50_000),
    )(*operands)
    out, gradient, spatial, temporal = pl.pallas_call(
        functools.partial(write, 3 * share),
        out_shape=(
            jax.ShapeDtypeStruct(images.shape, F32),
            jax.ShapeDtypeStruct(images.shape, F32),
            jax.ShapeDtypeStruct((3, 3 * share, chans), F32),
            jax.ShapeDtypeStruct((3 * share, chans), F32),
        ),
        in_specs=[vmem] * 3,
        out_specs=(hbm,) * 4,
        scratch_shapes=[pltpu.SemaphoreType.DMA((6,))],
        compiler_params=pltpu.CompilerParams(vmem_limit_bytes=VMEM_LIMIT),
        cost_estimate=pl.CostEstimate(flops=0, bytes_accessed=1_200_000, transcendentals=0),
    )(*results)
    return (
        out,
        gradient,
        spatial.reshape(3, 3, share, chans).transpose(0, 1, 3, 2),
        temporal.reshape(3, share, chans).transpose(0, 2, 1),
    )


def solution(mesh):
    return jax.shard_map(
        functools.partial(per_device, mesh.shape["frames"], mesh.shape["rows"]),
        mesh=mesh,
        in_specs=(P("frames", "rows", None, None), P(), P(), P("frames", "rows", None, None)),
        out_specs=(
            P("frames", "rows", None, None),
            P("frames", "rows", None, None),
            P(None, None, None, "rows"),
            P(None, None, "rows"),
        ),
        check_vma=False,
    )
```

```python
import functools
import math

import jax
import jax.numpy as jnp
from jax import lax
from jax.experimental import pallas as pl
from jax.experimental.pallas import tpu as pltpu
from jax.sharding import PartitionSpec as P

MESH = pl.DeviceIdType.MESH
F32, BF16 = jnp.float32, jnp.bfloat16
PER_CORE = 2
GROUPS = 6 // PER_CORE
VMEM_LIMIT = 24 * 2**20


def split(value):
    high = value.astype(BF16)
    return high, (value - high.astype(F32)).astype(BF16)


def dot(a, b):
    return jnp.dot(a, b, preferred_element_type=F32)


def put_weight(dst, index, value):
    high, low = split(value)
    n = value.shape[1]
    dst[index, :, :n] = high
    dst[index, :, n:] = low


def product(high, low, both):
    n = both.shape[1] // 2
    wide = dot(high, both)
    return wide[:, :n] + wide[:, n:] + dot(low, both[:, :n])


def put_row(dst, row, frames):
    width, chans = frames[0].shape
    at = lax.broadcasted_iota(jnp.int32, (width, chans), 0)
    for f, value in enumerate(frames):
        before = jnp.where(at == 0, 0.0, pltpu.roll(value, 1, 0))
        after = jnp.where(at == width - 1, 0.0, pltpu.roll(value, width - 1, 0))
        rows = pl.ds(f * width, width)
        for b, moved in enumerate((before, value, after)):
            high, low = split(moved)
            dst[row, rows, b * chans : (b + 1) * chans] = high
            dst[row, rows, (3 + b) * chans : (4 + b) * chans] = low


def kernel(
    nfd, nrd, share, piece, factor,
    x_hbm, sw_hbm, tw_hbm, cot_hbm, mix_ref, gi_ref, gr_ref,
    x_ref, sw_ref, tw_ref, cot_ref, load_sem, xs, ds, wf, wb, tf, tb, xhalo, chalo, ahalo, dhalo, act, dpre, cots, acts,
    terms, core_in, half, rows_in, plane, z_in, own, final, send_sem, recv_sem,
):
    nf, strip, width, chans = x_ref.shape
    assert nf == 2 and strip == 2
    wide = nf * width
    three = 3 * chans
    fr, ro = lax.axis_index("frames"), lax.axis_index("rows")
    core, z = lax.rem(fr, 2), lax.div(fr, 2)
    nz = nfd // 2
    other = fr + 1 - 2 * core
    n_sems = [0]
    sent = []

    def remote(src, dst, **where):
        n = n_sems[0]
        n_sems[0] += 1
        return pltpu.make_async_remote_copy(
            src_ref=src, dst_ref=dst, send_sem=send_sem.at[n], recv_sem=recv_sem.at[n],
            device_id=where, device_id_type=MESH,
        )

    def send(src, dst, **where):
        copy = remote(src, dst, **where)
        copy.start()
        sent.append(copy)
        return copy

    loads = [
        pltpu.make_async_copy(src, dst, load_sem.at[n])
        for n, (src, dst) in enumerate(
            ((x_hbm, x_ref), (cot_hbm, cot_ref), (tw_hbm, tw_ref), (sw_hbm, sw_ref))
        )
    ]
    for load in loads:
        load.start()
    barrier = pltpu.get_barrier_semaphore()
    for o in range(1, nrd):
        pl.semaphore_signal(barrier, inc=1, device_id={"rows": lax.rem(ro + o, nrd)}, device_id_type=MESH)
    for o in range(1, nfd):
        pl.semaphore_signal(barrier, inc=1, device_id={"frames": lax.rem(fr + o, nfd)}, device_id_type=MESH)

    pl.semaphore_wait(barrier, nrd - 1 + nfd - 1)

    has_up, has_down = ro > 0, ro < nrd - 1
    has_prev, has_next = fr > 0, fr < nfd - 1
    up, down = lax.rem(ro + nrd - 1, nrd), lax.rem(ro + 1, nrd)
    prev, following = lax.rem(fr + nfd - 1, nfd), lax.rem(fr + 1, nfd)
    x_up = remote(x_hbm.at[:, 0], xhalo.at[1], rows=up)
    x_down = remote(x_hbm.at[:, strip - 1], xhalo.at[0], rows=down)
    c_prev = remote(cot_hbm, chalo, frames=prev)
    a_next = remote(act, ahalo, frames=following)
    d_up = remote(dpre.at[0], dhalo.at[1], rows=up)
    d_down = remote(dpre.at[strip - 1], dhalo.at[0], rows=down)

    def receive(copy, there, zeroed):
        @pl.when(there)
        def _():
            copy.wait_recv()

        @pl.when(jnp.logical_not(there))
        def _():
            zeroed[...] = jnp.zeros(zeroed.shape, F32)

    @pl.when(has_up)
    def _():
        x_up.start()

    @pl.when(has_down)
    def _():
        x_down.start()

    @pl.when(has_prev)
    def _():
        c_prev.start()

    def put_cots(first, src):
        for f in range(nf):
            for h in range(strip):
                rows = pl.ds(first + f * width, width)
                high, low = split(src[f, h])
                cots[0, h, rows, :] = high
                cots[1, h, rows, :] = low

    loads[0].wait()
    for h in range(strip):
        put_row(xs, h + 1, [x_ref[f, h] for f in range(nf)])
    loads[1].wait()
    put_cots(0, cot_ref)
    loads[2].wait()
    for k in range(3):
        put_weight(tb, k, tw_ref[k].T)
    loads[3].wait()
    for i in range(3):
        put_weight(wf, i, sw_ref[i].reshape(three, chans))

    def conv(src, row, count, weight, i):
        rows = src[row : row + count].reshape(count * wide, 2 * three)
        return product(rows[:, :three], rows[:, three:], weight[i])

    middle = conv(xs, 1, 2, wf, 1)
    pre = [middle[:wide] + conv(xs, 2, 1, wf, 2), middle[wide:] + conv(xs, 1, 1, wf, 0)]

    def temporal(src, shift, weight, k):
        rows = pl.ds(shift * width, wide)
        both = [src[p, :, rows, :].reshape(strip * wide, chans) for p in range(2)]
        return product(both[0], both[1], weight[k])

    dact = temporal(cots, 0, tb, 0)
    receive(c_prev, has_next, chalo)
    put_cots(wide, chalo)
    dact = dact + temporal(cots, 1, tb, 1) + temporal(cots, 2, tb, 2)

    receive(x_down, has_up, xhalo.at[0])
    put_row(xs, 0, [xhalo[0, f] for f in range(nf)])
    receive(x_up, has_down, xhalo.at[1])
    put_row(xs, 3, [xhalo[1, f] for f in range(nf)])
    pre = [pre[0] + conv(xs, 0, 1, wf, 0), pre[1] + conv(xs, 3, 1, wf, 2)]

    both_act, both_dpre = [], []
    for h in range(strip):
        sig = 1.0 / (1.0 + jnp.exp(-pre[h]))
        act_h = pre[h] * sig
        act[h] = act_h
        dpre_h = dact[h * wide : (h + 1) * wide] * sig * (1.0 + pre[h] * (1.0 - sig))
        dpre[h] = dpre_h
        both_act.append(act_h)
        both_dpre.append(dpre_h)

    @pl.when(has_next)
    def _():
        a_next.start()

    def put_term(tap, value):
        g, place = divmod(tap, 2 * PER_CORE)
        terms[g, place // PER_CORE, place % PER_CORE] = value

    act_t = split(jnp.concatenate(both_act, axis=0).T)
    for k in range(3):
        rows = pl.ds(k * width, wide)
        c_high = cots[0, :, rows, :].reshape(strip * wide, chans)
        c_low = cots[1, :, rows, :].reshape(strip * wide, chans)
        term = dot(act_t[0], c_high) + dot(act_t[0], c_low) + dot(act_t[1], c_high)
        put_term(k, term.T)
    dpre_t = split(jnp.concatenate(both_dpre, axis=0).T)

    def spatial_terms(i, first):
        src = xs[i : i + strip].reshape(strip * wide, 2 * three)
        wide_term = dot(dpre_t[0], src)
        term = wide_term[:, :three] + wide_term[:, three:] + dot(dpre_t[1], src[:, :three])
        for j in range(3):
            put_term(first + j, term[:, j * chans : (j + 1) * chans])

    spatial_terms(1, 3)
    to_core = [None] * GROUPS
    to_rows = [None] * GROUPS
    to_z = [None] * GROUPS
    around_z = [None] * GROUPS
    back = [None] * GROUPS

    def start_core(g):
        to_core[g] = send(terms.at[g, 1 - core], core_in.at[g], frames=other)

    def start_rows(g):
        to_core[g].wait_recv()
        half[g] = terms[g, core] + core_in[g]
        to_rows[g] = []
        for o in range(1, nrd):
            target = lax.rem(ro + o, nrd)
            part = pl.ds(pl.multiple_of(target * share, 8), share)
            to_rows[g].append(send(half.at[g, :, part, :], rows_in.at[g, o - 1], rows=target))

    def start_z(g):
        total = half[g, :, pl.ds(pl.multiple_of(ro * share, 8), share), :]
        for o in range(1, nrd):
            to_rows[g][o - 1].wait_recv()
            total = total + rows_in[g, o - 1]
        plane[g, : PER_CORE * share] = total.reshape(PER_CORE * share, chans) * factor
        if nz * piece > PER_CORE * share:
            plane[g, PER_CORE * share :] = jnp.zeros((nz * piece - PER_CORE * share, chans), F32)
        to_z[g] = []
        for o in range(1, nz):
            target = lax.rem(z + o, nz)
            part = pl.ds(pl.multiple_of(target * piece, 8), piece)
            to_z[g].append(send(plane.at[g, part], z_in.at[g, o - 1], frames=2 * target + core))

    def start_around(g):
        mine = pl.ds(pl.multiple_of(z * piece, 8), piece)
        total = plane[g, mine]
        for o in range(1, nz):
            to_z[g][o - 1].wait_recv()
            total = total + z_in[g, o - 1]
        own[g, 0] = total
        final[g, core, mine] = total
        around_z[g] = []
        for o in range(1, nz):
            target = lax.rem(z + o, nz)
            around_z[g].append(send(own.at[g, 0], final.at[g, core, mine], frames=2 * target + core))

    def start_back(g):
        for copy in around_z[g]:
            copy.wait_recv()
        back[g] = send(final.at[g, core], final.at[g, core], frames=other)

    def finish(g):
        back[g].wait_recv()
        gr_ref[g] = final[g]

    def put_acts(first, src):
        for h in range(strip):
            high, low = split(src[h])
            acts[0, h, pl.ds(first, wide), :] = high
            acts[1, h, pl.ds(first, wide), :] = low

    start_core(0)
    spatial_terms(0, 6)
    start_core(1)
    start_rows(0)
    spatial_terms(2, 9)
    start_core(2)
    start_rows(1)
    for h in range(strip):
        put_row(ds, h + 1, [dpre[h, pl.ds(f * width, width)] for f in range(nf)])
    start_rows(2)

    @pl.when(has_up)
    def _():
        d_up.start()

    @pl.when(has_down)
    def _():
        d_down.start()

    for k in range(3):
        put_weight(tf, k, tw_ref[k])
    put_acts(wide, act)
    mixed = temporal(acts, 2, tf, 0)
    receive(a_next, has_prev, ahalo)
    put_acts(0, ahalo)
    start_z(0)
    mixed = mixed + temporal(acts, 1, tf, 1) + temporal(acts, 0, tf, 2)
    for h in range(strip):
        for f in range(nf):
            at = h * wide + f * width
            mix_ref[f, h] = x_ref[f, h] + mixed[at : at + width]
    start_z(1)

    for i in range(3):
        put_weight(wb, i, jnp.concatenate([sw_ref[i, 2 - b].T for b in range(3)], axis=0))
    start_around(0)
    start_z(2)
    middle = conv(ds, 1, 2, wb, 1)
    grad = [middle[:wide] + conv(ds, 2, 1, wb, 0), middle[wide:] + conv(ds, 1, 1, wb, 2)]
    start_around(1)
    start_back(0)
    receive(d_down, has_up, dhalo.at[0])
    put_row(ds, 0, [dhalo[0, pl.ds(f * width, width)] for f in range(nf)])
    receive(d_up, has_down, dhalo.at[1])
    put_row(ds, 3, [dhalo[1, pl.ds(f * width, width)] for f in range(nf)])
    start_around(2)
    start_back(1)
    grad = [grad[0] + conv(ds, 0, 1, wb, 2), grad[1] + conv(ds, 3, 1, wb, 0)]
    for h in range(strip):
        for f in range(nf):
            at = f * width
            gi_ref[f, h] = cot_ref[f, h] + grad[h][at : at + width]
    start_back(2)
    for g in range(GROUPS):
        finish(g)

    for copy in sent:
        copy.wait_send()
    for copy, there in (
        (x_up, has_up), (x_down, has_down), (c_prev, has_prev),
        (a_next, has_next), (d_up, has_up), (d_down, has_down),
    ):
        pl.when(there)(copy.wait_send)


def write(share, mix_ref, gi_ref, gr_ref, out_ref, grad_ref, spatial_ref, temporal_ref, sem):
    pairs = [(mix_ref, out_ref), (gi_ref, grad_ref)]
    for tap in range(12):
        g, place = divmod(tap, 2 * PER_CORE)
        src = gr_ref.at[g, place // PER_CORE, pl.ds(place % PER_CORE * share, share)]
        i = (1, 0, 2)[tap // 3 - 1]
        pairs.append((src, temporal_ref.at[tap] if tap < 3 else spatial_ref.at[i, tap % 3]))
    copies = [pltpu.make_async_copy(src, dst, sem.at[n]) for n, (src, dst) in enumerate(pairs)]
    for copy in copies:
        copy.start()
    for copy in copies:
        copy.wait()


def per_device(nfd, nrd, images, spatial_weight, temporal_weight, cotangent):
    nf, strip, width, chans = images.shape
    wide, three = nf * width, 3 * chans
    nz, share = nfd // 2, chans // nrd
    piece = -(-(PER_CORE * share) // nz)
    piece = -(-piece // 8) * 8
    factor = 1.0 / math.sqrt(nf * nfd * strip * nrd * width)
    n_sems = 6 + GROUPS * (2 + (nrd - 1) + 2 * (nz - 1))
    vmem, hbm = (pl.BlockSpec(memory_space=space) for space in (pltpu.VMEM, pltpu.HBM))
    operands = (images, spatial_weight, temporal_weight, cotangent)
    operands = [pltpu.with_memory_space_constraint(a, pltpu.HBM) for a in operands]
    results = pl.pallas_call(
        functools.partial(kernel, nfd, nrd, share, piece, factor),
        out_shape=(
            pltpu.VMEM(images.shape, F32),
            pltpu.VMEM(images.shape, F32),
            pltpu.VMEM((GROUPS, 2, nz * piece, chans), F32),
        ),
        in_specs=[hbm] * 4,
        out_specs=(vmem,) * 3,
        scratch_shapes=[
            *(pltpu.VMEM(a.shape, F32) for a in operands),
            pltpu.SemaphoreType.DMA((4,)),
            pltpu.VMEM((strip + 2, wide, 2 * three), BF16),
            pltpu.VMEM((strip + 2, wide, 2 * three), BF16),
            pltpu.VMEM((3, three, 2 * chans), BF16),
            pltpu.VMEM((3, three, 2 * chans), BF16),
            pltpu.VMEM((3, chans, 2 * chans), BF16),
            pltpu.VMEM((3, chans, 2 * chans), BF16),
            pltpu.VMEM((2, nf, width, chans), F32),
            pltpu.VMEM((nf, strip, width, chans), F32),
            pltpu.VMEM((strip, wide, chans), F32),
            pltpu.VMEM((2, wide, chans), F32),
            pltpu.VMEM((strip, wide, chans), F32),
            pltpu.VMEM((strip, wide, chans), F32),
            pltpu.VMEM((2, strip, 2 * wide, chans), BF16),
            pltpu.VMEM((2, strip, 2 * wide, chans), BF16),
            pltpu.VMEM((GROUPS, 2, PER_CORE, chans, chans), F32),
            pltpu.VMEM((GROUPS, PER_CORE, chans, chans), F32),
            pltpu.VMEM((GROUPS, PER_CORE, chans, chans), F32),
            pltpu.VMEM((GROUPS, nrd - 1, PER_CORE, share, chans), F32),
            pltpu.VMEM((GROUPS, nz * piece, chans), F32),
            pltpu.VMEM((GROUPS, nz - 1, piece, chans), F32),
            pltpu.VMEM((GROUPS, 1, piece, chans), F32),
            pltpu.VMEM((GROUPS, 2, nz * piece, chans), F32),
            pltpu.SemaphoreType.DMA((n_sems,)),
            pltpu.SemaphoreType.DMA((n_sems,)),
        ],
        compiler_params=pltpu.CompilerParams(
            collective_id=0, has_side_effects=True, vmem_limit_bytes=VMEM_LIMIT
        ),
        cost_estimate=pl.CostEstimate(flops=1_400_000_000, bytes_accessed=2_000_000, transcendentals=50_000),
    )(*operands)
    out, gradient, spatial, temporal = pl.pallas_call(
        functools.partial(write, share),
        out_shape=(
            jax.ShapeDtypeStruct(images.shape, F32),
            jax.ShapeDtypeStruct(images.shape, F32),
            jax.ShapeDtypeStruct((3, 3, share, chans), F32),
            jax.ShapeDtypeStruct((3, share, chans), F32),
        ),
        in_specs=[vmem] * 3,
        out_specs=(hbm,) * 4,
        scratch_shapes=[pltpu.SemaphoreType.DMA((14,))],
        compiler_params=pltpu.CompilerParams(vmem_limit_bytes=VMEM_LIMIT),
        cost_estimate=pl.CostEstimate(flops=0, bytes_accessed=1_200_000, transcendentals=0),
    )(*results)
    return (
        out,
        gradient,
        spatial.transpose(0, 1, 3, 2),
        temporal.transpose(0, 2, 1),
    )


def solution(mesh):
    return jax.shard_map(
        functools.partial(per_device, mesh.shape["frames"], mesh.shape["rows"]),
        mesh=mesh,
        in_specs=(P("frames", "rows", None, None), P(), P(), P("frames", "rows", None, None)),
        out_specs=(
            P("frames", "rows", None, None),
            P("frames", "rows", None, None),
            P(None, None, None, "rows"),
            P(None, None, "rows"),
        ),
        check_vma=False,
    )
```

```python
import functools
import math

import jax
import jax.numpy as jnp
from jax import lax
from jax.experimental import pallas as pl
from jax.experimental.pallas import tpu as pltpu
from jax.sharding import PartitionSpec as P

MESH = pl.DeviceIdType.MESH
F32, BF16 = jnp.float32, jnp.bfloat16
PER_CORE = 2
GROUPS = 6 // PER_CORE
VMEM_LIMIT = 24 * 2**20


def split(value):
    high = value.astype(BF16)
    return high, (value - high.astype(F32)).astype(BF16)


def dot(a, b):
    return jnp.dot(a, b, preferred_element_type=F32)


def put_weight(dst, index, value):
    high, low = split(value)
    n = value.shape[1]
    dst[index, :, :n] = high
    dst[index, :, n:] = low


def product(stacked, both):
    m, n = stacked.shape[0] // 2, both.shape[1] // 2
    wide = dot(stacked, both)
    return wide[:m, :n] + (wide[:m, n:] + wide[m:, :n] + wide[m:, n:])


def put_row(dst, row, frames):
    width, chans = frames[0].shape
    at = lax.broadcasted_iota(jnp.int32, (width, chans), 0)
    for f, value in enumerate(frames):
        before = jnp.where(at == 0, 0.0, pltpu.roll(value, 1, 0))
        after = jnp.where(at == width - 1, 0.0, pltpu.roll(value, width - 1, 0))
        rows = pl.ds(f * width, width)
        for b, moved in enumerate((before, value, after)):
            high, low = split(moved)
            dst[0, row, rows, b * chans : (b + 1) * chans] = high
            dst[1, row, rows, b * chans : (b + 1) * chans] = low


def kernel(
    nfd, nrd, share, piece, factor,
    x_hbm, sw_hbm, tw_hbm, cot_hbm, mix_ref, gi_ref, gr_ref,
    x_ref, sw_ref, tw_ref, cot_ref, load_sem, xs, ds, wf, wb, tf, tb, xhalo, chalo, ahalo, dhalo, act, dpre, cots, acts,
    terms, core_in, half, rows_in, plane, z_in, own, final, send_sem, recv_sem,
):
    nf, strip, width, chans = x_ref.shape
    assert nf == 2 and strip == 2
    wide = nf * width
    three = 3 * chans
    fr, ro = lax.axis_index("frames"), lax.axis_index("rows")
    core, z = lax.rem(fr, 2), lax.div(fr, 2)
    nz = nfd // 2
    other = fr + 1 - 2 * core
    n_sems = [0]
    sent = []

    def remote(src, dst, **where):
        n = n_sems[0]
        n_sems[0] += 1
        return pltpu.make_async_remote_copy(
            src_ref=src, dst_ref=dst, send_sem=send_sem.at[n], recv_sem=recv_sem.at[n],
            device_id=where, device_id_type=MESH,
        )

    def send(src, dst, **where):
        copy = remote(src, dst, **where)
        copy.start()
        sent.append(copy)
        return copy

    loads = [
        pltpu.make_async_copy(src, dst, load_sem.at[n])
        for n, (src, dst) in enumerate(
            ((x_hbm, x_ref), (cot_hbm, cot_ref), (tw_hbm, tw_ref), (sw_hbm, sw_ref))
        )
    ]
    for load in loads:
        load.start()
    barrier = pltpu.get_barrier_semaphore()
    for o in range(1, nrd):
        pl.semaphore_signal(barrier, inc=1, device_id={"rows": lax.rem(ro + o, nrd)}, device_id_type=MESH)
    for o in range(1, nfd):
        pl.semaphore_signal(barrier, inc=1, device_id={"frames": lax.rem(fr + o, nfd)}, device_id_type=MESH)

    pl.semaphore_wait(barrier, nrd - 1 + nfd - 1)

    has_up, has_down = ro > 0, ro < nrd - 1
    has_prev, has_next = fr > 0, fr < nfd - 1
    up, down = lax.rem(ro + nrd - 1, nrd), lax.rem(ro + 1, nrd)
    prev, following = lax.rem(fr + nfd - 1, nfd), lax.rem(fr + 1, nfd)
    x_up = remote(x_hbm.at[:, 0], xhalo.at[1], rows=up)
    x_down = remote(x_hbm.at[:, strip - 1], xhalo.at[0], rows=down)
    c_prev = remote(cot_hbm, chalo, frames=prev)
    a_next = remote(act, ahalo, frames=following)
    d_up = remote(dpre.at[0], dhalo.at[1], rows=up)
    d_down = remote(dpre.at[strip - 1], dhalo.at[0], rows=down)

    def receive(copy, there, zeroed):
        @pl.when(there)
        def _():
            copy.wait_recv()

        @pl.when(jnp.logical_not(there))
        def _():
            zeroed[...] = jnp.zeros(zeroed.shape, F32)

    @pl.when(has_up)
    def _():
        x_up.start()

    @pl.when(has_down)
    def _():
        x_down.start()

    @pl.when(has_prev)
    def _():
        c_prev.start()

    def put_cots(first, src):
        for f in range(nf):
            for h in range(strip):
                rows = pl.ds(first + f * width, width)
                high, low = split(src[f, h])
                cots[0, h, rows, :] = high
                cots[1, h, rows, :] = low

    loads[0].wait()
    for h in range(strip):
        put_row(xs, h + 1, [x_ref[f, h] for f in range(nf)])
    loads[1].wait()
    put_cots(0, cot_ref)
    loads[2].wait()
    for k in range(3):
        put_weight(tb, k, tw_ref[k].T)
    loads[3].wait()
    for i in range(3):
        put_weight(wf, i, sw_ref[i].reshape(three, chans))

    def conv(src, row, count, weight, i):
        return product(src[:, row : row + count].reshape(2 * count * wide, three), weight[i])

    middle = conv(xs, 1, 2, wf, 1)
    pre = [middle[:wide] + conv(xs, 2, 1, wf, 2), middle[wide:] + conv(xs, 1, 1, wf, 0)]

    def temporal(src, shift, weight, k):
        rows = pl.ds(shift * width, wide)
        return product(src[:, :, rows, :].reshape(2 * strip * wide, chans), weight[k])

    dact = temporal(cots, 0, tb, 0)
    receive(c_prev, has_next, chalo)
    put_cots(wide, chalo)
    dact = dact + temporal(cots, 1, tb, 1) + temporal(cots, 2, tb, 2)

    receive(x_down, has_up, xhalo.at[0])
    put_row(xs, 0, [xhalo[0, f] for f in range(nf)])
    receive(x_up, has_down, xhalo.at[1])
    put_row(xs, 3, [xhalo[1, f] for f in range(nf)])
    pre = [pre[0] + conv(xs, 0, 1, wf, 0), pre[1] + conv(xs, 3, 1, wf, 2)]

    both_act, both_dpre = [], []
    for h in range(strip):
        sig = 1.0 / (1.0 + jnp.exp(-pre[h]))
        act_h = pre[h] * sig
        act[h] = act_h
        dpre_h = dact[h * wide : (h + 1) * wide] * sig * (1.0 + pre[h] * (1.0 - sig))
        dpre[h] = dpre_h
        both_act.append(act_h)
        both_dpre.append(dpre_h)

    @pl.when(has_next)
    def _():
        a_next.start()

    def stack(strips):
        return jnp.concatenate(split(jnp.concatenate(strips, axis=0).T), axis=0)

    def put_term(tap, value):
        g, place = divmod(tap, 2 * PER_CORE)
        terms[g, place // PER_CORE, place % PER_CORE] = value

    act_t = stack(both_act)
    for k in range(3):
        rows = pl.ds(k * width, wide)
        both = [cots[p, :, rows, :].reshape(strip * wide, chans) for p in range(2)]
        put_term(k, product(act_t, jnp.concatenate(both, axis=1)).T)
    dpre_t = stack(both_dpre)

    def spatial_terms(i, first):
        both = [xs[p, i : i + strip].reshape(strip * wide, three) for p in range(2)]
        term = product(dpre_t, jnp.concatenate(both, axis=1))
        for j in range(3):
            put_term(first + j, term[:, j * chans : (j + 1) * chans])

    spatial_terms(1, 3)
    to_core = [None] * GROUPS
    to_rows = [None] * GROUPS
    to_z = [None] * GROUPS
    around_z = [None] * GROUPS
    back = [None] * GROUPS

    def start_core(g):
        to_core[g] = send(terms.at[g, 1 - core], core_in.at[g], frames=other)

    def start_rows(g):
        to_core[g].wait_recv()
        half[g] = terms[g, core] + core_in[g]
        to_rows[g] = []
        for o in range(1, nrd):
            target = lax.rem(ro + o, nrd)
            part = pl.ds(pl.multiple_of(target * share, 8), share)
            to_rows[g].append(send(half.at[g, :, part, :], rows_in.at[g, o - 1], rows=target))

    def start_z(g):
        total = half[g, :, pl.ds(pl.multiple_of(ro * share, 8), share), :]
        for o in range(1, nrd):
            to_rows[g][o - 1].wait_recv()
            total = total + rows_in[g, o - 1]
        plane[g, : PER_CORE * share] = total.reshape(PER_CORE * share, chans) * factor
        if nz * piece > PER_CORE * share:
            plane[g, PER_CORE * share :] = jnp.zeros((nz * piece - PER_CORE * share, chans), F32)
        to_z[g] = []
        for o in range(1, nz):
            target = lax.rem(z + o, nz)
            part = pl.ds(pl.multiple_of(target * piece, 8), piece)
            to_z[g].append(send(plane.at[g, part], z_in.at[g, o - 1], frames=2 * target + core))

    def start_around(g):
        mine = pl.ds(pl.multiple_of(z * piece, 8), piece)
        total = plane[g, mine]
        for o in range(1, nz):
            to_z[g][o - 1].wait_recv()
            total = total + z_in[g, o - 1]
        own[g, 0] = total
        final[g, core, mine] = total
        around_z[g] = []
        for o in range(1, nz):
            target = lax.rem(z + o, nz)
            around_z[g].append(send(own.at[g, 0], final.at[g, core, mine], frames=2 * target + core))

    def start_back(g):
        for copy in around_z[g]:
            copy.wait_recv()
        back[g] = send(final.at[g, core], final.at[g, core], frames=other)

    def finish(g):
        back[g].wait_recv()
        gr_ref[g] = final[g]

    def put_acts(first, src):
        for h in range(strip):
            high, low = split(src[h])
            acts[0, h, pl.ds(first, wide), :] = high
            acts[1, h, pl.ds(first, wide), :] = low

    start_core(0)
    spatial_terms(0, 6)
    start_core(1)
    start_rows(0)
    spatial_terms(2, 9)
    start_core(2)
    start_rows(1)
    for h in range(strip):
        put_row(ds, h + 1, [dpre[h, pl.ds(f * width, width)] for f in range(nf)])
    start_rows(2)

    @pl.when(has_up)
    def _():
        d_up.start()

    @pl.when(has_down)
    def _():
        d_down.start()

    for k in range(3):
        put_weight(tf, k, tw_ref[k])
    put_acts(wide, act)
    mixed = temporal(acts, 2, tf, 0)
    receive(a_next, has_prev, ahalo)
    put_acts(0, ahalo)
    start_z(0)
    mixed = mixed + temporal(acts, 1, tf, 1) + temporal(acts, 0, tf, 2)
    for h in range(strip):
        for f in range(nf):
            at = h * wide + f * width
            mix_ref[f, h] = x_ref[f, h] + mixed[at : at + width]
    start_z(1)

    for i in range(3):
        put_weight(wb, i, jnp.concatenate([sw_ref[i, 2 - b].T for b in range(3)], axis=0))
    start_around(0)
    start_z(2)
    middle = conv(ds, 1, 2, wb, 1)
    grad = [middle[:wide] + conv(ds, 2, 1, wb, 0), middle[wide:] + conv(ds, 1, 1, wb, 2)]
    start_around(1)
    start_back(0)
    receive(d_down, has_up, dhalo.at[0])
    put_row(ds, 0, [dhalo[0, pl.ds(f * width, width)] for f in range(nf)])
    receive(d_up, has_down, dhalo.at[1])
    put_row(ds, 3, [dhalo[1, pl.ds(f * width, width)] for f in range(nf)])
    start_around(2)
    start_back(1)
    grad = [grad[0] + conv(ds, 0, 1, wb, 2), grad[1] + conv(ds, 3, 1, wb, 0)]
    for h in range(strip):
        for f in range(nf):
            at = f * width
            gi_ref[f, h] = cot_ref[f, h] + grad[h][at : at + width]
    start_back(2)
    for g in range(GROUPS):
        finish(g)

    for copy in sent:
        copy.wait_send()
    for copy, there in (
        (x_up, has_up), (x_down, has_down), (c_prev, has_prev),
        (a_next, has_next), (d_up, has_up), (d_down, has_down),
    ):
        pl.when(there)(copy.wait_send)


def write(share, mix_ref, gi_ref, gr_ref, out_ref, grad_ref, spatial_ref, temporal_ref, sem):
    pairs = [(mix_ref, out_ref), (gi_ref, grad_ref)]
    for tap in range(12):
        g, place = divmod(tap, 2 * PER_CORE)
        src = gr_ref.at[g, place // PER_CORE, pl.ds(place % PER_CORE * share, share)]
        i = (1, 0, 2)[tap // 3 - 1]
        pairs.append((src, temporal_ref.at[tap] if tap < 3 else spatial_ref.at[i, tap % 3]))
    copies = [pltpu.make_async_copy(src, dst, sem.at[n]) for n, (src, dst) in enumerate(pairs)]
    for copy in copies:
        copy.start()
    for copy in copies:
        copy.wait()


def per_device(nfd, nrd, images, spatial_weight, temporal_weight, cotangent):
    nf, strip, width, chans = images.shape
    wide, three = nf * width, 3 * chans
    nz, share = nfd // 2, chans // nrd
    piece = -(-(PER_CORE * share) // nz)
    piece = -(-piece // 8) * 8
    factor = 1.0 / math.sqrt(nf * nfd * strip * nrd * width)
    n_sems = 6 + GROUPS * (2 + (nrd - 1) + 2 * (nz - 1))
    vmem, hbm = (pl.BlockSpec(memory_space=space) for space in (pltpu.VMEM, pltpu.HBM))
    operands = (images, spatial_weight, temporal_weight, cotangent)
    operands = [pltpu.with_memory_space_constraint(a, pltpu.HBM) for a in operands]
    results = pl.pallas_call(
        functools.partial(kernel, nfd, nrd, share, piece, factor),
        out_shape=(
            pltpu.VMEM(images.shape, F32),
            pltpu.VMEM(images.shape, F32),
            pltpu.VMEM((GROUPS, 2, nz * piece, chans), F32),
        ),
        in_specs=[hbm] * 4,
        out_specs=(vmem,) * 3,
        scratch_shapes=[
            *(pltpu.VMEM(a.shape, F32) for a in operands),
            pltpu.SemaphoreType.DMA((4,)),
            pltpu.VMEM((2, strip + 2, wide, three), BF16),
            pltpu.VMEM((2, strip + 2, wide, three), BF16),
            pltpu.VMEM((3, three, 2 * chans), BF16),
            pltpu.VMEM((3, three, 2 * chans), BF16),
            pltpu.VMEM((3, chans, 2 * chans), BF16),
            pltpu.VMEM((3, chans, 2 * chans), BF16),
            pltpu.VMEM((2, nf, width, chans), F32),
            pltpu.VMEM((nf, strip, width, chans), F32),
            pltpu.VMEM((strip, wide, chans), F32),
            pltpu.VMEM((2, wide, chans), F32),
            pltpu.VMEM((strip, wide, chans), F32),
            pltpu.VMEM((strip, wide, chans), F32),
            pltpu.VMEM((2, strip, 2 * wide, chans), BF16),
            pltpu.VMEM((2, strip, 2 * wide, chans), BF16),
            pltpu.VMEM((GROUPS, 2, PER_CORE, chans, chans), F32),
            pltpu.VMEM((GROUPS, PER_CORE, chans, chans), F32),
            pltpu.VMEM((GROUPS, PER_CORE, chans, chans), F32),
            pltpu.VMEM((GROUPS, nrd - 1, PER_CORE, share, chans), F32),
            pltpu.VMEM((GROUPS, nz * piece, chans), F32),
            pltpu.VMEM((GROUPS, nz - 1, piece, chans), F32),
            pltpu.VMEM((GROUPS, 1, piece, chans), F32),
            pltpu.VMEM((GROUPS, 2, nz * piece, chans), F32),
            pltpu.SemaphoreType.DMA((n_sems,)),
            pltpu.SemaphoreType.DMA((n_sems,)),
        ],
        compiler_params=pltpu.CompilerParams(
            collective_id=0, has_side_effects=True, vmem_limit_bytes=VMEM_LIMIT
        ),
        cost_estimate=pl.CostEstimate(flops=1_400_000_000, bytes_accessed=2_000_000, transcendentals=50_000),
    )(*operands)
    out, gradient, spatial, temporal = pl.pallas_call(
        functools.partial(write, share),
        out_shape=(
            jax.ShapeDtypeStruct(images.shape, F32),
            jax.ShapeDtypeStruct(images.shape, F32),
            jax.ShapeDtypeStruct((3, 3, share, chans), F32),
            jax.ShapeDtypeStruct((3, share, chans), F32),
        ),
        in_specs=[vmem] * 3,
        out_specs=(hbm,) * 4,
        scratch_shapes=[pltpu.SemaphoreType.DMA((14,))],
        compiler_params=pltpu.CompilerParams(vmem_limit_bytes=VMEM_LIMIT),
        cost_estimate=pl.CostEstimate(flops=0, bytes_accessed=1_200_000, transcendentals=0),
    )(*results)
    return (
        out,
        gradient,
        spatial.transpose(0, 1, 3, 2),
        temporal.transpose(0, 2, 1),
    )


def solution(mesh):
    return jax.shard_map(
        functools.partial(per_device, mesh.shape["frames"], mesh.shape["rows"]),
        mesh=mesh,
        in_specs=(P("frames", "rows", None, None), P(), P(), P("frames", "rows", None, None)),
        out_specs=(
            P("frames", "rows", None, None),
            P("frames", "rows", None, None),
            P(None, None, None, "rows"),
            P(None, None, "rows"),
        ),
        check_vma=False,
    )
```

```python
import functools
import math

import jax
import jax.numpy as jnp
from jax import lax
from jax.experimental import pallas as pl
from jax.experimental.pallas import tpu as pltpu
from jax.sharding import PartitionSpec as P

MESH = pl.DeviceIdType.MESH
F32, BF16 = jnp.float32, jnp.bfloat16
PER_CORE = 2
GROUPS = 6 // PER_CORE
VMEM_LIMIT = 24 * 2**20


def split(value):
    high = value.astype(BF16)
    return high, (value - high.astype(F32)).astype(BF16)


def dot(a, b):
    return jnp.dot(a, b, preferred_element_type=F32)


def put_weight(dst, index, value):
    high, low = split(value)
    n = value.shape[1]
    dst[index, :, :n] = high
    dst[index, :, n:] = low


def product(stacked, both):
    m, n = stacked.shape[0] // 2, both.shape[1] // 2
    wide = dot(stacked, both)
    return wide[:m, :n] + (wide[:m, n:] + wide[m:, :n] + wide[m:, n:])


def put_row(dst, row, frames):
    width, chans = frames[0].shape
    at = lax.broadcasted_iota(jnp.int32, (width, chans), 0)
    for f, value in enumerate(frames):
        before = jnp.where(at == 0, 0.0, pltpu.roll(value, 1, 0))
        after = jnp.where(at == width - 1, 0.0, pltpu.roll(value, width - 1, 0))
        rows = pl.ds(f * width, width)
        for b, moved in enumerate((before, value, after)):
            high, low = split(moved)
            dst[0, row, rows, b * chans : (b + 1) * chans] = high
            dst[1, row, rows, b * chans : (b + 1) * chans] = low


def kernel(
    nfd, nrd, share, piece, factor,
    x_hbm, sw_hbm, tw_hbm, cot_hbm, mix_ref, gi_ref, gr_ref,
    x_ref, sw_ref, tw_ref, cot_ref, load_sem, xs, ds, wf, wb, tf, tb, xhalo, chalo, ahalo, dhalo, act, dpre, cots, acts,
    terms, core_in, half, rows_in, plane, z_in, own, final, send_sem, recv_sem,
):
    nf, strip, width, chans = x_ref.shape
    assert nf == 2 and strip == 2
    wide = nf * width
    three = 3 * chans
    fr, ro = lax.axis_index("frames"), lax.axis_index("rows")
    core, z = lax.rem(fr, 2), lax.div(fr, 2)
    nz = nfd // 2
    other = fr + 1 - 2 * core
    n_sems = [0]
    sent = []

    def remote(src, dst, **where):
        n = n_sems[0]
        n_sems[0] += 1
        return pltpu.make_async_remote_copy(
            src_ref=src, dst_ref=dst, send_sem=send_sem.at[n], recv_sem=recv_sem.at[n],
            device_id=where, device_id_type=MESH,
        )

    def send(src, dst, **where):
        copy = remote(src, dst, **where)
        copy.start()
        sent.append(copy)
        return copy

    loads = [
        pltpu.make_async_copy(src, dst, load_sem.at[n])
        for n, (src, dst) in enumerate(
            ((x_hbm, x_ref), (cot_hbm, cot_ref), (tw_hbm, tw_ref), (sw_hbm, sw_ref))
        )
    ]
    for load in loads:
        load.start()
    barrier = pltpu.get_barrier_semaphore()
    for o in range(1, nrd):
        pl.semaphore_signal(barrier, inc=1, device_id={"rows": lax.rem(ro + o, nrd)}, device_id_type=MESH)
    for o in range(1, nfd):
        pl.semaphore_signal(barrier, inc=1, device_id={"frames": lax.rem(fr + o, nfd)}, device_id_type=MESH)

    pl.semaphore_wait(barrier, nrd - 1 + nfd - 1)

    has_up, has_down = ro > 0, ro < nrd - 1
    has_prev, has_next = fr > 0, fr < nfd - 1
    up, down = lax.rem(ro + nrd - 1, nrd), lax.rem(ro + 1, nrd)
    prev, following = lax.rem(fr + nfd - 1, nfd), lax.rem(fr + 1, nfd)
    x_up = remote(x_hbm.at[:, 0], xhalo.at[1], rows=up)
    x_down = remote(x_hbm.at[:, strip - 1], xhalo.at[0], rows=down)
    c_prev = remote(cot_hbm, chalo, frames=prev)
    a_next = remote(act, ahalo, frames=following)
    d_up = remote(dpre.at[0], dhalo.at[1], rows=up)
    d_down = remote(dpre.at[strip - 1], dhalo.at[0], rows=down)

    def receive(copy, there, zeroed):
        @pl.when(there)
        def _():
            copy.wait_recv()

        @pl.when(jnp.logical_not(there))
        def _():
            zeroed[...] = jnp.zeros(zeroed.shape, F32)

    @pl.when(has_up)
    def _():
        x_up.start()

    @pl.when(has_down)
    def _():
        x_down.start()

    @pl.when(has_prev)
    def _():
        c_prev.start()

    def put_cots(first, src):
        for f in range(nf):
            for h in range(strip):
                rows = pl.ds(first + f * width, width)
                high, low = split(src[f, h])
                cots[0, h, rows, :] = high
                cots[1, h, rows, :] = low

    loads[0].wait()
    for h in range(strip):
        put_row(xs, h + 1, [x_ref[f, h] for f in range(nf)])
    loads[1].wait()
    put_cots(0, cot_ref)
    loads[2].wait()
    for k in range(3):
        put_weight(tb, k, tw_ref[k].T)
    loads[3].wait()
    for i in range(3):
        put_weight(wf, i, sw_ref[i].reshape(three, chans))

    def conv(src, row, count, weight, i):
        return product(src[:, row : row + count].reshape(2 * count * wide, three), weight[i])

    middle = conv(xs, 1, 2, wf, 1)
    pre = [middle[:wide] + conv(xs, 2, 1, wf, 2), middle[wide:] + conv(xs, 1, 1, wf, 0)]

    def temporal(src, shift, weight, k):
        rows = pl.ds(shift * width, wide)
        return product(src[:, :, rows, :].reshape(2 * strip * wide, chans), weight[k])

    dact = temporal(cots, 0, tb, 0)
    receive(c_prev, has_next, chalo)
    put_cots(wide, chalo)
    dact = dact + temporal(cots, 1, tb, 1) + temporal(cots, 2, tb, 2)

    receive(x_down, has_up, xhalo.at[0])
    put_row(xs, 0, [xhalo[0, f] for f in range(nf)])
    receive(x_up, has_down, xhalo.at[1])
    put_row(xs, 3, [xhalo[1, f] for f in range(nf)])
    pre = [pre[0] + conv(xs, 0, 1, wf, 0), pre[1] + conv(xs, 3, 1, wf, 2)]

    both_act, both_dpre = [], []
    for h in range(strip):
        sig = 1.0 / (1.0 + jnp.exp(-pre[h]))
        act_h = pre[h] * sig
        act[h] = act_h
        dpre_h = dact[h * wide : (h + 1) * wide] * sig * (1.0 + pre[h] * (1.0 - sig))
        dpre[h] = dpre_h
        both_act.append(act_h)
        both_dpre.append(dpre_h)

    @pl.when(has_next)
    def _():
        a_next.start()

    def stack(strips):
        return jnp.concatenate(split(jnp.concatenate(strips, axis=0).T), axis=0)

    def put_term(tap, value):
        g, place = divmod(tap, 2 * PER_CORE)
        terms[g, place // PER_CORE, place % PER_CORE] = value

    act_t = stack(both_act)
    for k in range(3):
        rows = pl.ds(k * width, wide)
        both = [cots[p, :, rows, :].reshape(strip * wide, chans) for p in range(2)]
        put_term(k, product(act_t, jnp.concatenate(both, axis=1)).T)
    dpre_t = stack(both_dpre)

    def spatial_terms(i, first):
        both = [xs[p, i : i + strip].reshape(strip * wide, three) for p in range(2)]
        term = product(dpre_t, jnp.concatenate(both, axis=1))
        for j in range(3):
            put_term(first + j, term[:, j * chans : (j + 1) * chans])

    spatial_terms(1, 3)
    to_core = [None] * GROUPS
    to_rows = [None] * GROUPS
    to_z = [None] * GROUPS
    around_z = [None] * GROUPS
    back = [None] * GROUPS

    def start_core(g):
        to_core[g] = send(terms.at[g, 1 - core], core_in.at[g], frames=other)

    def start_rows(g):
        to_core[g].wait_recv()
        half[g] = terms[g, core] + core_in[g]
        to_rows[g] = []
        for o in range(1, nrd):
            target = lax.rem(ro + o, nrd)
            part = pl.ds(pl.multiple_of(target * share, 8), share)
            to_rows[g].append(send(half.at[g, :, part, :], rows_in.at[g, o - 1], rows=target))

    def start_z(g):
        total = half[g, :, pl.ds(pl.multiple_of(ro * share, 8), share), :]
        for o in range(1, nrd):
            to_rows[g][o - 1].wait_recv()
            total = total + rows_in[g, o - 1]
        plane[g, : PER_CORE * share] = total.reshape(PER_CORE * share, chans) * factor
        if nz * piece > PER_CORE * share:
            plane[g, PER_CORE * share :] = jnp.zeros((nz * piece - PER_CORE * share, chans), F32)
        to_z[g] = []
        for o in range(1, nz):
            target = lax.rem(z + o, nz)
            part = pl.ds(pl.multiple_of(target * piece, 8), piece)
            to_z[g].append(send(plane.at[g, part], z_in.at[g, o - 1], frames=2 * target + core))

    def start_around(g):
        mine = pl.ds(pl.multiple_of(z * piece, 8), piece)
        total = plane[g, mine]
        for o in range(1, nz):
            to_z[g][o - 1].wait_recv()
            total = total + z_in[g, o - 1]
        own[g, 0] = total
        final[g, core, mine] = total
        around_z[g] = []
        for o in range(1, nz):
            target = lax.rem(z + o, nz)
            around_z[g].append(send(own.at[g, 0], final.at[g, core, mine], frames=2 * target + core))

    def start_back(g):
        for copy in around_z[g]:
            copy.wait_recv()
        back[g] = send(final.at[g, core], final.at[g, core], frames=other)

    def finish(g):
        back[g].wait_recv()
        gr_ref[g] = final[g]

    def put_acts(first, src):
        for h in range(strip):
            high, low = split(src[h])
            acts[0, h, pl.ds(first, wide), :] = high
            acts[1, h, pl.ds(first, wide), :] = low

    start_core(0)
    spatial_terms(0, 6)
    start_core(1)
    start_rows(0)
    spatial_terms(2, 9)
    start_core(2)
    start_rows(1)
    start_rows(2)

    @pl.when(has_up)
    def _():
        d_up.start()

    @pl.when(has_down)
    def _():
        d_down.start()

    for k in range(3):
        put_weight(tf, k, tw_ref[k])
    put_acts(wide, act)
    start_z(0)
    mixed = temporal(acts, 2, tf, 0)
    receive(a_next, has_prev, ahalo)
    put_acts(0, ahalo)
    mixed = mixed + temporal(acts, 1, tf, 1) + temporal(acts, 0, tf, 2)
    for h in range(strip):
        for f in range(nf):
            at = h * wide + f * width
            mix_ref[f, h] = x_ref[f, h] + mixed[at : at + width]
    start_z(1)
    for h in range(strip):
        put_row(ds, h + 1, [dpre[h, pl.ds(f * width, width)] for f in range(nf)])
    start_around(0)
    for i in range(3):
        put_weight(wb, i, jnp.concatenate([sw_ref[i, 2 - b].T for b in range(3)], axis=0))
    start_z(2)
    start_around(1)
    middle = conv(ds, 1, 2, wb, 1)
    grad = [middle[:wide] + conv(ds, 2, 1, wb, 0), middle[wide:] + conv(ds, 1, 1, wb, 2)]
    start_back(0)
    start_around(2)
    start_back(1)
    start_back(2)
    receive(d_down, has_up, dhalo.at[0])
    put_row(ds, 0, [dhalo[0, pl.ds(f * width, width)] for f in range(nf)])
    receive(d_up, has_down, dhalo.at[1])
    put_row(ds, 3, [dhalo[1, pl.ds(f * width, width)] for f in range(nf)])
    grad = [grad[0] + conv(ds, 0, 1, wb, 2), grad[1] + conv(ds, 3, 1, wb, 0)]
    for h in range(strip):
        for f in range(nf):
            at = f * width
            gi_ref[f, h] = cot_ref[f, h] + grad[h][at : at + width]
    for g in range(GROUPS):
        finish(g)

    for copy in sent:
        copy.wait_send()
    for copy, there in (
        (x_up, has_up), (x_down, has_down), (c_prev, has_prev),
        (a_next, has_next), (d_up, has_up), (d_down, has_down),
    ):
        pl.when(there)(copy.wait_send)


def write(share, mix_ref, gi_ref, gr_ref, out_ref, grad_ref, spatial_ref, temporal_ref, sem):
    pairs = [(mix_ref, out_ref), (gi_ref, grad_ref)]
    for tap in range(12):
        g, place = divmod(tap, 2 * PER_CORE)
        src = gr_ref.at[g, place // PER_CORE, pl.ds(place % PER_CORE * share, share)]
        i = (1, 0, 2)[tap // 3 - 1]
        pairs.append((src, temporal_ref.at[tap] if tap < 3 else spatial_ref.at[i, tap % 3]))
    copies = [pltpu.make_async_copy(src, dst, sem.at[n]) for n, (src, dst) in enumerate(pairs)]
    for copy in copies:
        copy.start()
    for copy in copies:
        copy.wait()


def per_device(nfd, nrd, images, spatial_weight, temporal_weight, cotangent):
    nf, strip, width, chans = images.shape
    wide, three = nf * width, 3 * chans
    nz, share = nfd // 2, chans // nrd
    piece = -(-(PER_CORE * share) // nz)
    piece = -(-piece // 8) * 8
    factor = 1.0 / math.sqrt(nf * nfd * strip * nrd * width)
    n_sems = 6 + GROUPS * (2 + (nrd - 1) + 2 * (nz - 1))
    vmem, hbm = (pl.BlockSpec(memory_space=space) for space in (pltpu.VMEM, pltpu.HBM))
    operands = (images, spatial_weight, temporal_weight, cotangent)
    operands = [pltpu.with_memory_space_constraint(a, pltpu.HBM) for a in operands]
    results = pl.pallas_call(
        functools.partial(kernel, nfd, nrd, share, piece, factor),
        out_shape=(
            pltpu.VMEM(images.shape, F32),
            pltpu.VMEM(images.shape, F32),
            pltpu.VMEM((GROUPS, 2, nz * piece, chans), F32),
        ),
        in_specs=[hbm] * 4,
        out_specs=(vmem,) * 3,
        scratch_shapes=[
            *(pltpu.VMEM(a.shape, F32) for a in operands),
            pltpu.SemaphoreType.DMA((4,)),
            pltpu.VMEM((2, strip + 2, wide, three), BF16),
            pltpu.VMEM((2, strip + 2, wide, three), BF16),
            pltpu.VMEM((3, three, 2 * chans), BF16),
            pltpu.VMEM((3, three, 2 * chans), BF16),
            pltpu.VMEM((3, chans, 2 * chans), BF16),
            pltpu.VMEM((3, chans, 2 * chans), BF16),
            pltpu.VMEM((2, nf, width, chans), F32),
            pltpu.VMEM((nf, strip, width, chans), F32),
            pltpu.VMEM((strip, wide, chans), F32),
            pltpu.VMEM((2, wide, chans), F32),
            pltpu.VMEM((strip, wide, chans), F32),
            pltpu.VMEM((strip, wide, chans), F32),
            pltpu.VMEM((2, strip, 2 * wide, chans), BF16),
            pltpu.VMEM((2, strip, 2 * wide, chans), BF16),
            pltpu.VMEM((GROUPS, 2, PER_CORE, chans, chans), F32),
            pltpu.VMEM((GROUPS, PER_CORE, chans, chans), F32),
            pltpu.VMEM((GROUPS, PER_CORE, chans, chans), F32),
            pltpu.VMEM((GROUPS, nrd - 1, PER_CORE, share, chans), F32),
            pltpu.VMEM((GROUPS, nz * piece, chans), F32),
            pltpu.VMEM((GROUPS, nz - 1, piece, chans), F32),
            pltpu.VMEM((GROUPS, 1, piece, chans), F32),
            pltpu.VMEM((GROUPS, 2, nz * piece, chans), F32),
            pltpu.SemaphoreType.DMA((n_sems,)),
            pltpu.SemaphoreType.DMA((n_sems,)),
        ],
        compiler_params=pltpu.CompilerParams(
            collective_id=0, has_side_effects=True, vmem_limit_bytes=VMEM_LIMIT
        ),
        cost_estimate=pl.CostEstimate(flops=1_400_000_000, bytes_accessed=2_000_000, transcendentals=50_000),
    )(*operands)
    out, gradient, spatial, temporal = pl.pallas_call(
        functools.partial(write, share),
        out_shape=(
            jax.ShapeDtypeStruct(images.shape, F32),
            jax.ShapeDtypeStruct(images.shape, F32),
            jax.ShapeDtypeStruct((3, 3, share, chans), F32),
            jax.ShapeDtypeStruct((3, share, chans), F32),
        ),
        in_specs=[vmem] * 3,
        out_specs=(hbm,) * 4,
        scratch_shapes=[pltpu.SemaphoreType.DMA((14,))],
        compiler_params=pltpu.CompilerParams(vmem_limit_bytes=VMEM_LIMIT),
        cost_estimate=pl.CostEstimate(flops=0, bytes_accessed=1_200_000, transcendentals=0),
    )(*results)
    return (
        out,
        gradient,
        spatial.transpose(0, 1, 3, 2),
        temporal.transpose(0, 2, 1),
    )


def solution(mesh):
    return jax.shard_map(
        functools.partial(per_device, mesh.shape["frames"], mesh.shape["rows"]),
        mesh=mesh,
        in_specs=(P("frames", "rows", None, None), P(), P(), P("frames", "rows", None, None)),
        out_specs=(
            P("frames", "rows", None, None),
            P("frames", "rows", None, None),
            P(None, None, None, "rows"),
            P(None, None, "rows"),
        ),
        check_vma=False,
    )
```

```python
import functools
import math

import jax
import jax.numpy as jnp
from jax import lax
from jax.experimental import pallas as pl
from jax.experimental.pallas import tpu as pltpu
from jax.sharding import PartitionSpec as P

MESH = pl.DeviceIdType.MESH
F32, BF16 = jnp.float32, jnp.bfloat16
PER_CORE = 3
GROUPS = 6 // PER_CORE
VMEM_LIMIT = 24 * 2**20


def split(value):
    high = value.astype(BF16)
    return high, (value - high.astype(F32)).astype(BF16)


def dot(a, b):
    return jnp.dot(a, b, preferred_element_type=F32)


def put_weight(dst, index, value):
    high, low = split(value)
    n = value.shape[1]
    dst[index, :, :n] = high
    dst[index, :, n:] = low


def product(stacked, both):
    m, n = stacked.shape[0] // 2, both.shape[1] // 2
    wide = dot(stacked, both)
    return wide[:m, :n] + (wide[:m, n:] + wide[m:, :n] + wide[m:, n:])


def put_row(dst, row, frames):
    width, chans = frames[0].shape
    at = lax.broadcasted_iota(jnp.int32, (width, chans), 0)
    for f, value in enumerate(frames):
        before = jnp.where(at == 0, 0.0, pltpu.roll(value, 1, 0))
        after = jnp.where(at == width - 1, 0.0, pltpu.roll(value, width - 1, 0))
        rows = pl.ds(f * width, width)
        for b, moved in enumerate((before, value, after)):
            high, low = split(moved)
            dst[0, row, rows, b * chans : (b + 1) * chans] = high
            dst[1, row, rows, b * chans : (b + 1) * chans] = low


def kernel(
    nfd, nrd, share, piece, factor,
    x_hbm, sw_hbm, tw_hbm, cot_hbm, mix_ref, gi_ref, gr_ref,
    x_ref, sw_ref, tw_ref, cot_ref, load_sem, xs, ds, wf, wb, tf, tb, xhalo, chalo, ahalo, dhalo, act, dpre, cots, acts,
    terms, core_in, half, rows_in, plane, z_in, own, final, send_sem, recv_sem,
):
    nf, strip, width, chans = x_ref.shape
    assert nf == 2 and strip == 2
    wide = nf * width
    three = 3 * chans
    fr, ro = lax.axis_index("frames"), lax.axis_index("rows")
    core, z = lax.rem(fr, 2), lax.div(fr, 2)
    nz = nfd // 2
    other = fr + 1 - 2 * core
    n_sems = [0]
    sent = []

    def remote(src, dst, **where):
        n = n_sems[0]
        n_sems[0] += 1
        return pltpu.make_async_remote_copy(
            src_ref=src, dst_ref=dst, send_sem=send_sem.at[n], recv_sem=recv_sem.at[n],
            device_id=where, device_id_type=MESH,
        )

    def send(src, dst, **where):
        copy = remote(src, dst, **where)
        copy.start()
        sent.append(copy)
        return copy

    loads = [
        pltpu.make_async_copy(src, dst, load_sem.at[n])
        for n, (src, dst) in enumerate(
            ((x_hbm, x_ref), (cot_hbm, cot_ref), (tw_hbm, tw_ref), (sw_hbm, sw_ref))
        )
    ]
    for load in loads:
        load.start()
    for halo in (xhalo, chalo, ahalo, dhalo):
        halo[...] = jnp.zeros(halo.shape, F32)
    barrier = pltpu.get_barrier_semaphore()
    for o in range(1, nrd):
        pl.semaphore_signal(barrier, inc=1, device_id={"rows": lax.rem(ro + o, nrd)}, device_id_type=MESH)
    for o in range(1, nfd):
        pl.semaphore_signal(barrier, inc=1, device_id={"frames": lax.rem(fr + o, nfd)}, device_id_type=MESH)

    pl.semaphore_wait(barrier, nrd - 1 + nfd - 1)

    has_up, has_down = ro > 0, ro < nrd - 1
    has_prev, has_next = fr > 0, fr < nfd - 1
    up, down = lax.rem(ro + nrd - 1, nrd), lax.rem(ro + 1, nrd)
    prev, following = lax.rem(fr + nfd - 1, nfd), lax.rem(fr + 1, nfd)
    x_up = remote(x_hbm.at[:, 0], xhalo.at[1], rows=up)
    x_down = remote(x_hbm.at[:, strip - 1], xhalo.at[0], rows=down)
    c_prev = remote(cot_hbm, chalo, frames=prev)
    a_next = remote(act, ahalo, frames=following)
    d_up = remote(dpre.at[0], dhalo.at[1], rows=up)
    d_down = remote(dpre.at[strip - 1], dhalo.at[0], rows=down)

    def receive(copy, there):
        @pl.when(there)
        def _():
            copy.wait_recv()

    @pl.when(has_up)
    def _():
        x_up.start()

    @pl.when(has_down)
    def _():
        x_down.start()

    @pl.when(has_prev)
    def _():
        c_prev.start()

    def put_cots(first, src):
        for f in range(nf):
            for h in range(strip):
                rows = pl.ds(first + f * width, width)
                high, low = split(src[f, h])
                cots[0, h, rows, :] = high
                cots[1, h, rows, :] = low

    loads[0].wait()
    for h in range(strip):
        put_row(xs, h + 1, [x_ref[f, h] for f in range(nf)])
    loads[1].wait()
    put_cots(0, cot_ref)
    loads[2].wait()
    for k in range(3):
        put_weight(tb, k, tw_ref[k].T)
    loads[3].wait()
    for i in range(3):
        put_weight(wf, i, sw_ref[i].reshape(three, chans))

    def conv(src, row, count, weight, i):
        return product(src[:, row : row + count].reshape(2 * count * wide, three), weight[i])

    middle = conv(xs, 1, 2, wf, 1)
    pre = [middle[:wide] + conv(xs, 2, 1, wf, 2), middle[wide:] + conv(xs, 1, 1, wf, 0)]

    def temporal(src, shift, weight, k):
        rows = pl.ds(shift * width, wide)
        return product(src[:, :, rows, :].reshape(2 * strip * wide, chans), weight[k])

    dact = temporal(cots, 0, tb, 0)
    receive(c_prev, has_next)
    put_cots(wide, chalo)
    dact = dact + temporal(cots, 1, tb, 1) + temporal(cots, 2, tb, 2)

    receive(x_down, has_up)
    put_row(xs, 0, [xhalo[0, f] for f in range(nf)])
    receive(x_up, has_down)
    put_row(xs, 3, [xhalo[1, f] for f in range(nf)])
    pre = [pre[0] + conv(xs, 0, 1, wf, 0), pre[1] + conv(xs, 3, 1, wf, 2)]

    both_act, both_dpre = [], []
    for h in range(strip):
        sig = 1.0 / (1.0 + jnp.exp(-pre[h]))
        act_h = pre[h] * sig
        act[h] = act_h
        dpre_h = dact[h * wide : (h + 1) * wide] * sig * (1.0 + pre[h] * (1.0 - sig))
        dpre[h] = dpre_h
        both_act.append(act_h)
        both_dpre.append(dpre_h)

    @pl.when(has_next)
    def _():
        a_next.start()

    def stack(strips):
        return jnp.concatenate(split(jnp.concatenate(strips, axis=0).T), axis=0)

    def put_term(tap, value):
        g, place = divmod(tap, 2 * PER_CORE)
        terms[g, place // PER_CORE, place % PER_CORE] = value

    act_t = stack(both_act)
    for k in range(3):
        rows = pl.ds(k * width, wide)
        both = [cots[p, :, rows, :].reshape(strip * wide, chans) for p in range(2)]
        put_term(k, product(act_t, jnp.concatenate(both, axis=1)).T)
    dpre_t = stack(both_dpre)

    def spatial_terms(i, first):
        both = [xs[p, i : i + strip].reshape(strip * wide, three) for p in range(2)]
        term = product(dpre_t, jnp.concatenate(both, axis=1))
        for j in range(3):
            put_term(first + j, term[:, j * chans : (j + 1) * chans])

    spatial_terms(1, 3)
    to_core = [None] * GROUPS
    to_rows = [None] * GROUPS
    to_z = [None] * GROUPS
    around_z = [None] * GROUPS
    back = [None] * GROUPS

    def start_core(g):
        to_core[g] = send(terms.at[g, 1 - core], core_in.at[g], frames=other)

    def start_rows(g):
        to_core[g].wait_recv()
        half[g] = terms[g, core] + core_in[g]
        to_rows[g] = []
        for o in range(1, nrd):
            target = lax.rem(ro + o, nrd)
            part = pl.ds(pl.multiple_of(target * share, 8), share)
            to_rows[g].append(send(half.at[g, :, part, :], rows_in.at[g, o - 1], rows=target))

    def start_z(g):
        total = half[g, :, pl.ds(pl.multiple_of(ro * share, 8), share), :]
        for copy in to_rows[g]:
            copy.wait_recv()
        for o in range(1, nrd):
            total = total + rows_in[g, o - 1]
        plane[g, : PER_CORE * share] = total.reshape(PER_CORE * share, chans) * factor
        if nz * piece > PER_CORE * share:
            plane[g, PER_CORE * share :] = jnp.zeros((nz * piece - PER_CORE * share, chans), F32)
        to_z[g] = []
        for o in range(1, nz):
            target = lax.rem(z + o, nz)
            part = pl.ds(pl.multiple_of(target * piece, 8), piece)
            to_z[g].append(send(plane.at[g, part], z_in.at[g, o - 1], frames=2 * target + core))

    def start_around(g):
        mine = pl.ds(pl.multiple_of(z * piece, 8), piece)
        total = plane[g, mine]
        for copy in to_z[g]:
            copy.wait_recv()
        for o in range(1, nz):
            total = total + z_in[g, o - 1]
        own[g, 0] = total
        final[g, core, mine] = total
        around_z[g] = []
        for o in range(1, nz):
            target = lax.rem(z + o, nz)
            around_z[g].append(send(own.at[g, 0], final.at[g, core, mine], frames=2 * target + core))

    def start_back(g):
        for copy in around_z[g]:
            copy.wait_recv()
        back[g] = send(final.at[g, core], final.at[g, core], frames=other)

    def finish(g):
        back[g].wait_recv()
        gr_ref[g] = final[g]

    def put_acts(first, src):
        for h in range(strip):
            high, low = split(src[h])
            acts[0, h, pl.ds(first, wide), :] = high
            acts[1, h, pl.ds(first, wide), :] = low

    start_core(0)
    spatial_terms(0, 6)
    spatial_terms(2, 9)
    start_core(1)
    start_rows(0)
    start_rows(1)

    @pl.when(has_up)
    def _():
        d_up.start()

    @pl.when(has_down)
    def _():
        d_down.start()

    for k in range(3):
        put_weight(tf, k, tw_ref[k])
    put_acts(wide, act)
    mixed = temporal(acts, 2, tf, 0)
    receive(a_next, has_prev)
    put_acts(0, ahalo)
    mixed = mixed + temporal(acts, 1, tf, 1) + temporal(acts, 0, tf, 2)
    for h in range(strip):
        for f in range(nf):
            at = h * wide + f * width
            mix_ref[f, h] = x_ref[f, h] + mixed[at : at + width]
    start_z(0)
    for h in range(strip):
        put_row(ds, h + 1, [dpre[h, pl.ds(f * width, width)] for f in range(nf)])
    start_z(1)
    start_around(0)
    for i in range(3):
        put_weight(wb, i, jnp.concatenate([sw_ref[i, 2 - b].T for b in range(3)], axis=0))
    start_around(1)
    start_back(0)
    middle = conv(ds, 1, 2, wb, 1)
    grad = [middle[:wide] + conv(ds, 2, 1, wb, 0), middle[wide:] + conv(ds, 1, 1, wb, 2)]
    start_back(1)
    receive(d_down, has_up)
    put_row(ds, 0, [dhalo[0, pl.ds(f * width, width)] for f in range(nf)])
    receive(d_up, has_down)
    put_row(ds, 3, [dhalo[1, pl.ds(f * width, width)] for f in range(nf)])
    grad = [grad[0] + conv(ds, 0, 1, wb, 2), grad[1] + conv(ds, 3, 1, wb, 0)]
    for h in range(strip):
        for f in range(nf):
            at = f * width
            gi_ref[f, h] = cot_ref[f, h] + grad[h][at : at + width]
    for g in range(GROUPS):
        finish(g)

    for copy in sent:
        copy.wait_send()
    for copy, there in (
        (x_up, has_up), (x_down, has_down), (c_prev, has_prev),
        (a_next, has_next), (d_up, has_up), (d_down, has_down),
    ):
        pl.when(there)(copy.wait_send)


def write(share, mix_ref, gi_ref, gr_ref, out_ref, grad_ref, spatial_ref, temporal_ref, sem):
    pairs = [(mix_ref, out_ref), (gi_ref, grad_ref)]
    for tap in range(12):
        g, place = divmod(tap, 2 * PER_CORE)
        src = gr_ref.at[g, place // PER_CORE, pl.ds(place % PER_CORE * share, share)]
        i = (1, 0, 2)[tap // 3 - 1]
        pairs.append((src, temporal_ref.at[tap] if tap < 3 else spatial_ref.at[i, tap % 3]))
    copies = [pltpu.make_async_copy(src, dst, sem.at[n]) for n, (src, dst) in enumerate(pairs)]
    for copy in copies:
        copy.start()
    for copy in copies:
        copy.wait()


def per_device(nfd, nrd, images, spatial_weight, temporal_weight, cotangent):
    nf, strip, width, chans = images.shape
    wide, three = nf * width, 3 * chans
    nz, share = nfd // 2, chans // nrd
    piece = -(-(PER_CORE * share) // nz)
    piece = -(-piece // 8) * 8
    factor = 1.0 / math.sqrt(nf * nfd * strip * nrd * width)
    n_sems = 6 + GROUPS * (2 + (nrd - 1) + 2 * (nz - 1))
    vmem, hbm = (pl.BlockSpec(memory_space=space) for space in (pltpu.VMEM, pltpu.HBM))
    operands = (images, spatial_weight, temporal_weight, cotangent)
    operands = [pltpu.with_memory_space_constraint(a, pltpu.HBM) for a in operands]
    results = pl.pallas_call(
        functools.partial(kernel, nfd, nrd, share, piece, factor),
        out_shape=(
            pltpu.VMEM(images.shape, F32),
            pltpu.VMEM(images.shape, F32),
            pltpu.VMEM((GROUPS, 2, nz * piece, chans), F32),
        ),
        in_specs=[hbm] * 4,
        out_specs=(vmem,) * 3,
        scratch_shapes=[
            *(pltpu.VMEM(a.shape, F32) for a in operands),
            pltpu.SemaphoreType.DMA((4,)),
            pltpu.VMEM((2, strip + 2, wide, three), BF16),
            pltpu.VMEM((2, strip + 2, wide, three), BF16),
            pltpu.VMEM((3, three, 2 * chans), BF16),
            pltpu.VMEM((3, three, 2 * chans), BF16),
            pltpu.VMEM((3, chans, 2 * chans), BF16),
            pltpu.VMEM((3, chans, 2 * chans), BF16),
            pltpu.VMEM((2, nf, width, chans), F32),
            pltpu.VMEM((nf, strip, width, chans), F32),
            pltpu.VMEM((strip, wide, chans), F32),
            pltpu.VMEM((2, wide, chans), F32),
            pltpu.VMEM((strip, wide, chans), F32),
            pltpu.VMEM((strip, wide, chans), F32),
            pltpu.VMEM((2, strip, 2 * wide, chans), BF16),
            pltpu.VMEM((2, strip, 2 * wide, chans), BF16),
            pltpu.VMEM((GROUPS, 2, PER_CORE, chans, chans), F32),
            pltpu.VMEM((GROUPS, PER_CORE, chans, chans), F32),
            pltpu.VMEM((GROUPS, PER_CORE, chans, chans), F32),
            pltpu.VMEM((GROUPS, nrd - 1, PER_CORE, share, chans), F32),
            pltpu.VMEM((GROUPS, nz * piece, chans), F32),
            pltpu.VMEM((GROUPS, nz - 1, piece, chans), F32),
            pltpu.VMEM((GROUPS, 1, piece, chans), F32),
            pltpu.VMEM((GROUPS, 2, nz * piece, chans), F32),
            pltpu.SemaphoreType.DMA((n_sems,)),
            pltpu.SemaphoreType.DMA((n_sems,)),
        ],
        compiler_params=pltpu.CompilerParams(
            collective_id=0, has_side_effects=True, vmem_limit_bytes=VMEM_LIMIT
        ),
        cost_estimate=pl.CostEstimate(flops=1_400_000_000, bytes_accessed=2_000_000, transcendentals=50_000),
    )(*operands)
    out, gradient, spatial, temporal = pl.pallas_call(
        functools.partial(write, share),
        out_shape=(
            jax.ShapeDtypeStruct(images.shape, F32),
            jax.ShapeDtypeStruct(images.shape, F32),
            jax.ShapeDtypeStruct((3, 3, share, chans), F32),
            jax.ShapeDtypeStruct((3, share, chans), F32),
        ),
        in_specs=[vmem] * 3,
        out_specs=(hbm,) * 4,
        scratch_shapes=[pltpu.SemaphoreType.DMA((14,))],
        compiler_params=pltpu.CompilerParams(vmem_limit_bytes=VMEM_LIMIT),
        cost_estimate=pl.CostEstimate(flops=0, bytes_accessed=1_200_000, transcendentals=0),
    )(*results)
    return (
        out,
        gradient,
        spatial.transpose(0, 1, 3, 2),
        temporal.transpose(0, 2, 1),
    )


def solution(mesh):
    return jax.shard_map(
        functools.partial(per_device, mesh.shape["frames"], mesh.shape["rows"]),
        mesh=mesh,
        in_specs=(P("frames", "rows", None, None), P(), P(), P("frames", "rows", None, None)),
        out_specs=(
            P("frames", "rows", None, None),
            P("frames", "rows", None, None),
            P(None, None, None, "rows"),
            P(None, None, "rows"),
        ),
        check_vma=False,
    )
```

```python
import functools
import math

import jax
import jax.numpy as jnp
from jax import lax
from jax.experimental import pallas as pl
from jax.experimental.pallas import tpu as pltpu
from jax.sharding import PartitionSpec as P

MESH = pl.DeviceIdType.MESH
F32, BF16 = jnp.float32, jnp.bfloat16
PER_CORE = 3
GROUPS = 6 // PER_CORE
VMEM_LIMIT = 24 * 2**20


def split(value):
    high = value.astype(BF16)
    return high, (value - high.astype(F32)).astype(BF16)


def dot(a, b):
    return jnp.dot(a, b, preferred_element_type=F32)


def put_weight(dst, index, value):
    high, low = split(value)
    n = value.shape[1]
    dst[index, :, :n] = high
    dst[index, :, n:] = low


def product(stacked, both):
    m, n = stacked.shape[0] // 2, both.shape[1] // 2
    wide = dot(stacked, both)
    return wide[:m, :n] + (wide[:m, n:] + wide[m:, :n] + wide[m:, n:])


def put_row(dst, row, frames):
    width, chans = frames[0].shape
    at = lax.broadcasted_iota(jnp.int32, (width, chans), 0)
    for f, value in enumerate(frames):
        before = jnp.where(at == 0, 0.0, pltpu.roll(value, 1, 0))
        after = jnp.where(at == width - 1, 0.0, pltpu.roll(value, width - 1, 0))
        rows = pl.ds(f * width, width)
        for b, moved in enumerate((before, value, after)):
            high, low = split(moved)
            dst[0, row, rows, b * chans : (b + 1) * chans] = high
            dst[1, row, rows, b * chans : (b + 1) * chans] = low


def kernel(
    nfd, nrd, share, piece, factor,
    x_hbm, sw_hbm, tw_hbm, cot_hbm, mix_ref, gi_ref, gr_ref,
    x_ref, sw_ref, tw_ref, cot_ref, load_sem, xs, ds, wf, wb, tf, tb, xhalo, chalo, ahalo, dhalo, act, dpre, cots, acts,
    terms, core_in, half, rows_in, passed, plane, z_in, own, final, send_sem, recv_sem,
):
    nf, strip, width, chans = x_ref.shape
    assert nf == 2 and strip == 2
    wide = nf * width
    three = 3 * chans
    fr, ro = lax.axis_index("frames"), lax.axis_index("rows")
    core, z = lax.rem(fr, 2), lax.div(fr, 2)
    nz = nfd // 2
    other = fr + 1 - 2 * core
    n_sems = [0]
    sent = []

    def remote(src, dst, **where):
        n = n_sems[0]
        n_sems[0] += 1
        return pltpu.make_async_remote_copy(
            src_ref=src, dst_ref=dst, send_sem=send_sem.at[n], recv_sem=recv_sem.at[n],
            device_id=where, device_id_type=MESH,
        )

    def send(src, dst, **where):
        copy = remote(src, dst, **where)
        copy.start()
        sent.append(copy)
        return copy

    loads = [
        pltpu.make_async_copy(src, dst, load_sem.at[n])
        for n, (src, dst) in enumerate(
            ((x_hbm, x_ref), (cot_hbm, cot_ref), (tw_hbm, tw_ref), (sw_hbm, sw_ref))
        )
    ]
    for load in loads:
        load.start()
    for halo in (xhalo, chalo, ahalo, dhalo):
        halo[...] = jnp.zeros(halo.shape, F32)
    barrier = pltpu.get_barrier_semaphore()
    for o in range(1, nrd):
        pl.semaphore_signal(barrier, inc=1, device_id={"rows": lax.rem(ro + o, nrd)}, device_id_type=MESH)
    for o in range(1, nfd):
        pl.semaphore_signal(barrier, inc=1, device_id={"frames": lax.rem(fr + o, nfd)}, device_id_type=MESH)

    pl.semaphore_wait(barrier, nrd - 1 + nfd - 1)

    has_up, has_down = ro > 0, ro < nrd - 1
    has_prev, has_next = fr > 0, fr < nfd - 1
    up, down = lax.rem(ro + nrd - 1, nrd), lax.rem(ro + 1, nrd)
    prev, following = lax.rem(fr + nfd - 1, nfd), lax.rem(fr + 1, nfd)
    x_up = remote(x_hbm.at[:, 0], xhalo.at[1], rows=up)
    x_down = remote(x_hbm.at[:, strip - 1], xhalo.at[0], rows=down)
    c_prev = remote(cot_hbm, chalo, frames=prev)
    a_next = remote(act, ahalo, frames=following)
    d_up = remote(dpre.at[0], dhalo.at[1], rows=up)
    d_down = remote(dpre.at[strip - 1], dhalo.at[0], rows=down)

    def receive(copy, there):
        @pl.when(there)
        def _():
            copy.wait_recv()

    @pl.when(has_up)
    def _():
        x_up.start()

    @pl.when(has_down)
    def _():
        x_down.start()

    @pl.when(has_prev)
    def _():
        c_prev.start()

    def put_cots(first, src):
        for f in range(nf):
            for h in range(strip):
                rows = pl.ds(first + f * width, width)
                high, low = split(src[f, h])
                cots[0, h, rows, :] = high
                cots[1, h, rows, :] = low

    loads[0].wait()
    for h in range(strip):
        put_row(xs, h + 1, [x_ref[f, h] for f in range(nf)])
    loads[1].wait()
    put_cots(0, cot_ref)
    loads[2].wait()
    for k in range(3):
        put_weight(tb, k, tw_ref[k].T)
    loads[3].wait()
    for i in range(3):
        put_weight(wf, i, sw_ref[i].reshape(three, chans))

    def conv(src, row, count, weight, i):
        return product(src[:, row : row + count].reshape(2 * count * wide, three), weight[i])

    middle = conv(xs, 1, 2, wf, 1)
    pre = [middle[:wide] + conv(xs, 2, 1, wf, 2), middle[wide:] + conv(xs, 1, 1, wf, 0)]

    def temporal(src, shift, weight, k):
        rows = pl.ds(shift * width, wide)
        return product(src[:, :, rows, :].reshape(2 * strip * wide, chans), weight[k])

    dact = temporal(cots, 0, tb, 0)
    receive(c_prev, has_next)
    put_cots(wide, chalo)
    dact = dact + temporal(cots, 1, tb, 1) + temporal(cots, 2, tb, 2)

    receive(x_down, has_up)
    put_row(xs, 0, [xhalo[0, f] for f in range(nf)])
    receive(x_up, has_down)
    put_row(xs, 3, [xhalo[1, f] for f in range(nf)])
    pre = [pre[0] + conv(xs, 0, 1, wf, 0), pre[1] + conv(xs, 3, 1, wf, 2)]

    both_act, both_dpre = [], []
    for h in range(strip):
        sig = 1.0 / (1.0 + jnp.exp(-pre[h]))
        act_h = pre[h] * sig
        act[h] = act_h
        dpre_h = dact[h * wide : (h + 1) * wide] * sig * (1.0 + pre[h] * (1.0 - sig))
        dpre[h] = dpre_h
        both_act.append(act_h)
        both_dpre.append(dpre_h)

    @pl.when(has_next)
    def _():
        a_next.start()

    def stack(strips):
        return jnp.concatenate(split(jnp.concatenate(strips, axis=0).T), axis=0)

    def put_term(tap, value):
        g, place = divmod(tap, 2 * PER_CORE)
        terms[g, place // PER_CORE, place % PER_CORE] = value

    act_t = stack(both_act)
    for k in range(3):
        rows = pl.ds(k * width, wide)
        both = [cots[p, :, rows, :].reshape(strip * wide, chans) for p in range(2)]
        put_term(k, product(act_t, jnp.concatenate(both, axis=1)).T)
    dpre_t = stack(both_dpre)

    def spatial_terms(i, first):
        both = [xs[p, i : i + strip].reshape(strip * wide, three) for p in range(2)]
        term = product(dpre_t, jnp.concatenate(both, axis=1))
        for j in range(3):
            put_term(first + j, term[:, j * chans : (j + 1) * chans])

    spatial_terms(1, 3)
    two_steps = nrd == 4
    along = ro + 1 - 2 * lax.rem(ro, 2)
    across = ro + 2 - 4 * lax.div(ro, 2)
    first = along * (1 - core) + across * core
    second = across * (1 - core) + along * core

    def rows_of(target):
        return pl.ds(pl.multiple_of(target * share, 8), share)

    to_core = [None] * GROUPS
    to_rows = [None] * GROUPS
    to_z = [None] * GROUPS
    around_z = [None] * GROUPS
    back = [None] * GROUPS

    def start_core(g):
        to_core[g] = send(terms.at[g, 1 - core], core_in.at[g], frames=other)

    def start_rows(g):
        to_core[g].wait_recv()
        half[g] = terms[g, core] + core_in[g]
        if two_steps:
            to_rows[g] = [
                send(half.at[g, :, rows_of(nrd - 1 - ro), :], rows_in.at[g, 1], rows=first),
                send(half.at[g, :, rows_of(first), :], rows_in.at[g, 0], rows=first),
            ]
            return
        to_rows[g] = []
        for o in range(1, nrd):
            target = lax.rem(ro + o, nrd)
            to_rows[g].append(send(half.at[g, :, rows_of(target), :], rows_in.at[g, o - 1], rows=target))

    def forward_rows(g):
        if two_steps:
            to_rows[g].pop(0).wait_recv()
            passed[g] = half[g, :, rows_of(second), :] + rows_in[g, 1]
            to_rows[g].append(send(passed.at[g], rows_in.at[g, 2], rows=second))

    def start_z(g):
        total = half[g, :, rows_of(ro), :]
        for copy in to_rows[g]:
            copy.wait_recv()
        for o in (0, 2) if two_steps else range(nrd - 1):
            total = total + rows_in[g, o]
        plane[g, : PER_CORE * share] = total.reshape(PER_CORE * share, chans) * factor
        if nz * piece > PER_CORE * share:
            plane[g, PER_CORE * share :] = jnp.zeros((nz * piece - PER_CORE * share, chans), F32)
        to_z[g] = []
        for o in range(1, nz):
            target = lax.rem(z + o, nz)
            part = pl.ds(pl.multiple_of(target * piece, 8), piece)
            to_z[g].append(send(plane.at[g, part], z_in.at[g, o - 1], frames=2 * target + core))

    def start_around(g):
        mine = pl.ds(pl.multiple_of(z * piece, 8), piece)
        total = plane[g, mine]
        for copy in to_z[g]:
            copy.wait_recv()
        for o in range(1, nz):
            total = total + z_in[g, o - 1]
        own[g, 0] = total
        final[g, core, mine] = total
        around_z[g] = []
        for o in range(1, nz):
            target = lax.rem(z + o, nz)
            around_z[g].append(send(own.at[g, 0], final.at[g, core, mine], frames=2 * target + core))

    def start_back(g):
        for copy in around_z[g]:
            copy.wait_recv()
        back[g] = send(final.at[g, core], final.at[g, core], frames=other)

    def finish(g):
        back[g].wait_recv()
        gr_ref[g] = final[g]

    def put_acts(first, src):
        for h in range(strip):
            high, low = split(src[h])
            acts[0, h, pl.ds(first, wide), :] = high
            acts[1, h, pl.ds(first, wide), :] = low

    start_core(0)
    spatial_terms(0, 6)
    spatial_terms(2, 9)
    start_core(1)
    start_rows(0)
    start_rows(1)

    for k in range(3):
        put_weight(tf, k, tw_ref[k])
    put_acts(wide, act)
    forward_rows(0)
    mixed = temporal(acts, 2, tf, 0)
    forward_rows(1)

    @pl.when(has_up)
    def _():
        d_up.start()

    @pl.when(has_down)
    def _():
        d_down.start()

    receive(a_next, has_prev)
    put_acts(0, ahalo)
    mixed = mixed + temporal(acts, 1, tf, 1) + temporal(acts, 0, tf, 2)
    for h in range(strip):
        for f in range(nf):
            at = h * wide + f * width
            mix_ref[f, h] = x_ref[f, h] + mixed[at : at + width]
    start_z(0)
    for h in range(strip):
        put_row(ds, h + 1, [dpre[h, pl.ds(f * width, width)] for f in range(nf)])
    start_z(1)
    start_around(0)
    for i in range(3):
        put_weight(wb, i, jnp.concatenate([sw_ref[i, 2 - b].T for b in range(3)], axis=0))
    start_around(1)
    start_back(0)
    middle = conv(ds, 1, 2, wb, 1)
    grad = [middle[:wide] + conv(ds, 2, 1, wb, 0), middle[wide:] + conv(ds, 1, 1, wb, 2)]
    start_back(1)
    receive(d_down, has_up)
    put_row(ds, 0, [dhalo[0, pl.ds(f * width, width)] for f in range(nf)])
    receive(d_up, has_down)
    put_row(ds, 3, [dhalo[1, pl.ds(f * width, width)] for f in range(nf)])
    grad = [grad[0] + conv(ds, 0, 1, wb, 2), grad[1] + conv(ds, 3, 1, wb, 0)]
    for h in range(strip):
        for f in range(nf):
            at = f * width
            gi_ref[f, h] = cot_ref[f, h] + grad[h][at : at + width]
    for g in range(GROUPS):
        finish(g)

    for copy in sent:
        copy.wait_send()
    for copy, there in (
        (x_up, has_up), (x_down, has_down), (c_prev, has_prev),
        (a_next, has_next), (d_up, has_up), (d_down, has_down),
    ):
        pl.when(there)(copy.wait_send)


def write(share, mix_ref, gi_ref, gr_ref, out_ref, grad_ref, spatial_ref, temporal_ref, sem):
    pairs = [(mix_ref, out_ref), (gi_ref, grad_ref)]
    for tap in range(12):
        g, place = divmod(tap, 2 * PER_CORE)
        src = gr_ref.at[g, place // PER_CORE, pl.ds(place % PER_CORE * share, share)]
        i = (1, 0, 2)[tap // 3 - 1]
        pairs.append((src, temporal_ref.at[tap] if tap < 3 else spatial_ref.at[i, tap % 3]))
    copies = [pltpu.make_async_copy(src, dst, sem.at[n]) for n, (src, dst) in enumerate(pairs)]
    for copy in copies:
        copy.start()
    for copy in copies:
        copy.wait()


def per_device(nfd, nrd, images, spatial_weight, temporal_weight, cotangent):
    nf, strip, width, chans = images.shape
    wide, three = nf * width, 3 * chans
    nz, share = nfd // 2, chans // nrd
    piece = -(-(PER_CORE * share) // nz)
    piece = -(-piece // 8) * 8
    factor = 1.0 / math.sqrt(nf * nfd * strip * nrd * width)
    n_sems = 6 + GROUPS * (2 + (nrd - 1) + 2 * (nz - 1))
    vmem, hbm = (pl.BlockSpec(memory_space=space) for space in (pltpu.VMEM, pltpu.HBM))
    operands = (images, spatial_weight, temporal_weight, cotangent)
    operands = [pltpu.with_memory_space_constraint(a, pltpu.HBM) for a in operands]
    results = pl.pallas_call(
        functools.partial(kernel, nfd, nrd, share, piece, factor),
        out_shape=(
            pltpu.VMEM(images.shape, F32),
            pltpu.VMEM(images.shape, F32),
            pltpu.VMEM((GROUPS, 2, nz * piece, chans), F32),
        ),
        in_specs=[hbm] * 4,
        out_specs=(vmem,) * 3,
        scratch_shapes=[
            *(pltpu.VMEM(a.shape, F32) for a in operands),
            pltpu.SemaphoreType.DMA((4,)),
            pltpu.VMEM((2, strip + 2, wide, three), BF16),
            pltpu.VMEM((2, strip + 2, wide, three), BF16),
            pltpu.VMEM((3, three, 2 * chans), BF16),
            pltpu.VMEM((3, three, 2 * chans), BF16),
            pltpu.VMEM((3, chans, 2 * chans), BF16),
            pltpu.VMEM((3, chans, 2 * chans), BF16),
            pltpu.VMEM((2, nf, width, chans), F32),
            pltpu.VMEM((nf, strip, width, chans), F32),
            pltpu.VMEM((strip, wide, chans), F32),
            pltpu.VMEM((2, wide, chans), F32),
            pltpu.VMEM((strip, wide, chans), F32),
            pltpu.VMEM((strip, wide, chans), F32),
            pltpu.VMEM((2, strip, 2 * wide, chans), BF16),
            pltpu.VMEM((2, strip, 2 * wide, chans), BF16),
            pltpu.VMEM((GROUPS, 2, PER_CORE, chans, chans), F32),
            pltpu.VMEM((GROUPS, PER_CORE, chans, chans), F32),
            pltpu.VMEM((GROUPS, PER_CORE, chans, chans), F32),
            pltpu.VMEM((GROUPS, nrd - 1, PER_CORE, share, chans), F32),
            pltpu.VMEM((GROUPS, PER_CORE, share, chans), F32),
            pltpu.VMEM((GROUPS, nz * piece, chans), F32),
            pltpu.VMEM((GROUPS, nz - 1, piece, chans), F32),
            pltpu.VMEM((GROUPS, 1, piece, chans), F32),
            pltpu.VMEM((GROUPS, 2, nz * piece, chans), F32),
            pltpu.SemaphoreType.DMA((n_sems,)),
            pltpu.SemaphoreType.DMA((n_sems,)),
        ],
        compiler_params=pltpu.CompilerParams(
            collective_id=0, has_side_effects=True, vmem_limit_bytes=VMEM_LIMIT
        ),
        cost_estimate=pl.CostEstimate(flops=1_400_000_000, bytes_accessed=2_000_000, transcendentals=50_000),
    )(*operands)
    out, gradient, spatial, temporal = pl.pallas_call(
        functools.partial(write, share),
        out_shape=(
            jax.ShapeDtypeStruct(images.shape, F32),
            jax.ShapeDtypeStruct(images.shape, F32),
            jax.ShapeDtypeStruct((3, 3, share, chans), F32),
            jax.ShapeDtypeStruct((3, share, chans), F32),
        ),
        in_specs=[vmem] * 3,
        out_specs=(hbm,) * 4,
        scratch_shapes=[pltpu.SemaphoreType.DMA((14,))],
        compiler_params=pltpu.CompilerParams(vmem_limit_bytes=VMEM_LIMIT),
        cost_estimate=pl.CostEstimate(flops=0, bytes_accessed=1_200_000, transcendentals=0),
    )(*results)
    return (
        out,
        gradient,
        spatial.transpose(0, 1, 3, 2),
        temporal.transpose(0, 2, 1),
    )


def solution(mesh):
    return jax.shard_map(
        functools.partial(per_device, mesh.shape["frames"], mesh.shape["rows"]),
        mesh=mesh,
        in_specs=(P("frames", "rows", None, None), P(), P(), P("frames", "rows", None, None)),
        out_specs=(
            P("frames", "rows", None, None),
            P("frames", "rows", None, None),
            P(None, None, None, "rows"),
            P(None, None, "rows"),
        ),
        check_vma=False,
    )
```

```python
import functools
import math

import jax
import jax.numpy as jnp
from jax import lax
from jax.experimental import pallas as pl
from jax.experimental.pallas import tpu as pltpu
from jax.sharding import PartitionSpec as P

MESH = pl.DeviceIdType.MESH
F32, BF16 = jnp.float32, jnp.bfloat16
PER_CORE = 3
GROUPS = 6 // PER_CORE
VMEM_LIMIT = 24 * 2**20


def split(value):
    high = value.astype(BF16)
    return high, (value - high.astype(F32)).astype(BF16)


def dot(a, b):
    return jnp.dot(a, b, preferred_element_type=F32)


def put_weight(dst, index, value):
    high, low = split(value)
    n = value.shape[1]
    dst[index, :, :n] = high
    dst[index, :, n:] = low


def product(stacked, both):
    m, n = stacked.shape[0] // 2, both.shape[1] // 2
    wide = dot(stacked, both)
    return wide[:m, :n] + (wide[:m, n:] + wide[m:, :n] + wide[m:, n:])


def put_row(dst, row, f, value):
    width, chans = value.shape
    at = lax.broadcasted_iota(jnp.int32, (width, chans), 0)
    before = jnp.where(at == 0, 0.0, pltpu.roll(value, 1, 0))
    after = jnp.where(at == width - 1, 0.0, pltpu.roll(value, width - 1, 0))
    rows = frame_rows(f, width)
    for b, moved in enumerate((before, value, after)):
        high, low = split(moved)
        dst[0, row, rows, b * chans : (b + 1) * chans] = high
        dst[1, row, rows, b * chans : (b + 1) * chans] = low


def frame_rows(f, width, count=1):
    return pl.ds(pl.multiple_of(f * width, 32), count * width)


def each(count, body):
    lax.fori_loop(0, count, lambda n, _: (body(n), 0)[1], 0)


def kernel(
    nfd, nrd, share, piece, factor,
    x_hbm, sw_hbm, tw_hbm, cot_hbm, mix_ref, gi_ref, gr_ref,
    x_ref, sw_ref, tw_ref, cot_ref, load_sem, pre, dact, act_t, dpre_t, xs, ds, wf, wb, tf, tb, xhalo, chalo, ahalo, dhalo, act, dpre, cots, acts,
    terms, core_in, half, rows_in, plane, z_in, own, final, send_sem, recv_sem,
):
    nf, strip, width, chans = x_ref.shape
    assert nf == 2 and strip == 2
    wide = nf * width
    three = 3 * chans
    fr, ro = lax.axis_index("frames"), lax.axis_index("rows")
    core, z = lax.rem(fr, 2), lax.div(fr, 2)
    nz = nfd // 2
    other = fr + 1 - 2 * core
    n_sems = [0]
    sent = []

    def remote(src, dst, **where):
        n = n_sems[0]
        n_sems[0] += 1
        return pltpu.make_async_remote_copy(
            src_ref=src, dst_ref=dst, send_sem=send_sem.at[n], recv_sem=recv_sem.at[n],
            device_id=where, device_id_type=MESH,
        )

    def send(src, dst, **where):
        copy = remote(src, dst, **where)
        copy.start()
        sent.append(copy)
        return copy

    loads = [
        pltpu.make_async_copy(src, dst, load_sem.at[n])
        for n, (src, dst) in enumerate(
            ((x_hbm, x_ref), (cot_hbm, cot_ref), (tw_hbm, tw_ref), (sw_hbm, sw_ref))
        )
    ]
    for load in loads:
        load.start()
    for halo in (xhalo, chalo, ahalo, dhalo):
        halo[...] = jnp.zeros(halo.shape, F32)
    barrier = pltpu.get_barrier_semaphore()
    for o in range(1, nrd):
        pl.semaphore_signal(barrier, inc=1, device_id={"rows": lax.rem(ro + o, nrd)}, device_id_type=MESH)
    for o in range(1, nfd):
        pl.semaphore_signal(barrier, inc=1, device_id={"frames": lax.rem(fr + o, nfd)}, device_id_type=MESH)

    pl.semaphore_wait(barrier, nrd - 1 + nfd - 1)

    has_up, has_down = ro > 0, ro < nrd - 1
    has_prev, has_next = fr > 0, fr < nfd - 1
    up, down = lax.rem(ro + nrd - 1, nrd), lax.rem(ro + 1, nrd)
    prev, following = lax.rem(fr + nfd - 1, nfd), lax.rem(fr + 1, nfd)
    x_up = remote(x_hbm.at[:, 0], xhalo.at[1], rows=up)
    x_down = remote(x_hbm.at[:, strip - 1], xhalo.at[0], rows=down)
    c_prev = remote(cot_hbm, chalo, frames=prev)
    a_next = remote(act, ahalo, frames=following)
    d_up = remote(dpre.at[0], dhalo.at[1], rows=up)
    d_down = remote(dpre.at[strip - 1], dhalo.at[0], rows=down)

    def receive(copy, there):
        @pl.when(there)
        def _():
            copy.wait_recv()

    @pl.when(has_up)
    def _():
        x_up.start()

    @pl.when(has_down)
    def _():
        x_down.start()

    @pl.when(has_prev)
    def _():
        c_prev.start()

    assert width % 32 == 0

    def pair(n):
        return lax.div(n, 2), lax.rem(n, 2)

    def put_cots(first, src):
        def one(n):
            h, f = pair(n)
            high, low = split(src[f, h])
            rows = frame_rows(first + f, width)
            cots[0, h, rows, :] = high
            cots[1, h, rows, :] = low

        each(strip * nf, one)

    def conv(src, weight, dst, flip):
        dst[...] = jnp.zeros(dst.shape, F32)

        def one(i):
            rows = src[:, pl.ds(2 - i if flip else i, strip)]
            dst[...] += product(rows.reshape(2 * strip * wide, three), weight[i])

        each(3, one)

    def temporal(src, weight, dst, flip):
        dst[...] = jnp.zeros(dst.shape, F32)

        def one(k):
            rows = src[:, :, frame_rows(2 - k if flip else k, width, nf), :]
            dst[...] += product(rows.reshape(2 * strip * wide, chans), weight[k])

        each(3, one)

    loads[0].wait()

    def x_row(n):
        h, f = pair(n)
        put_row(xs, h + 1, f, x_ref[f, h])

    each(strip * nf, x_row)
    loads[1].wait()
    put_cots(0, cot_ref)
    loads[2].wait()

    def t_weights(k):
        put_weight(tb, k, tw_ref[k].T)
        put_weight(tf, k, tw_ref[k])

    each(3, t_weights)
    loads[3].wait()
    each(3, lambda i: put_weight(wf, i, sw_ref[i].reshape(three, chans)))
    receive(c_prev, has_next)
    put_cots(nf, chalo)
    temporal(cots, tb, dact, False)
    receive(x_down, has_up)
    receive(x_up, has_down)

    def x_edge(n):
        side, f = pair(n)
        put_row(xs, side * (strip + 1), f, xhalo[side, f])

    each(2 * nf, x_edge)
    conv(xs, wf, pre, False)

    def gates(h):
        rows = frame_rows(h, wide)
        value = pre[rows]
        sig = 1.0 / (1.0 + jnp.exp(-value))
        act[h] = value * sig
        dpre[h] = dact[rows] * sig * (1.0 + value * (1.0 - sig))

    each(strip, gates)

    @pl.when(has_next)
    def _():
        a_next.start()

    for dst, src in ((act_t, act), (dpre_t, dpre)):
        high, low = split(src[...].reshape(strip * wide, chans).T)
        dst[:chans] = high
        dst[chans:] = low

    def temporal_terms(k):
        both = [cots[p, :, frame_rows(k, width, nf), :].reshape(strip * wide, chans) for p in range(2)]
        terms[k] = product(act_t[...], jnp.concatenate(both, axis=1)).T

    def spatial_terms(i):
        both = [xs[p, pl.ds(i, strip)].reshape(strip * wide, three) for p in range(2)]
        term = product(dpre_t[...], jnp.concatenate(both, axis=1))
        for j in range(3):
            terms[3 * i + 3 + j] = term[:, j * chans : (j + 1) * chans]

    each(3, temporal_terms)
    each(3, spatial_terms)
    to_core = [None] * GROUPS
    to_rows = [None] * GROUPS
    to_z = [None] * GROUPS
    around_z = [None] * GROUPS
    back = [None] * GROUPS

    def start_core(g):
        to_core[g] = send(terms.at[pl.ds((2 * g + 1 - core) * PER_CORE, PER_CORE)], core_in.at[g], frames=other)

    def start_rows(g):
        to_core[g].wait_recv()
        half[g] = terms[pl.ds((2 * g + core) * PER_CORE, PER_CORE)] + core_in[g]
        to_rows[g] = []
        for o in range(1, nrd):
            target = lax.rem(ro + o, nrd)
            part = pl.ds(pl.multiple_of(target * share, 8), share)
            to_rows[g].append(send(half.at[g, :, part, :], rows_in.at[g, o - 1], rows=target))

    def start_z(g):
        total = half[g, :, pl.ds(pl.multiple_of(ro * share, 8), share), :]
        for copy in to_rows[g]:
            copy.wait_recv()
        for o in range(1, nrd):
            total = total + rows_in[g, o - 1]
        plane[g, : PER_CORE * share] = total.reshape(PER_CORE * share, chans) * factor
        if nz * piece > PER_CORE * share:
            plane[g, PER_CORE * share :] = jnp.zeros((nz * piece - PER_CORE * share, chans), F32)
        to_z[g] = []
        for o in range(1, nz):
            target = lax.rem(z + o, nz)
            part = pl.ds(pl.multiple_of(target * piece, 8), piece)
            to_z[g].append(send(plane.at[g, part], z_in.at[g, o - 1], frames=2 * target + core))

    def start_around(g):
        mine = pl.ds(pl.multiple_of(z * piece, 8), piece)
        total = plane[g, mine]
        for copy in to_z[g]:
            copy.wait_recv()
        for o in range(1, nz):
            total = total + z_in[g, o - 1]
        own[g, 0] = total
        final[g, core, mine] = total
        around_z[g] = []
        for o in range(1, nz):
            target = lax.rem(z + o, nz)
            around_z[g].append(send(own.at[g, 0], final.at[g, core, mine], frames=2 * target + core))

    def start_back(g):
        for copy in around_z[g]:
            copy.wait_recv()
        back[g] = send(final.at[g, core], final.at[g, core], frames=other)

    def finish(g):
        back[g].wait_recv()
        gr_ref[g] = final[g]

    def put_acts(first, src):
        def one(h):
            high, low = split(src[h])
            acts[0, h, pl.ds(first, wide), :] = high
            acts[1, h, pl.ds(first, wide), :] = low

        each(strip, one)

    start_core(0)
    start_core(1)
    start_rows(0)
    start_rows(1)

    @pl.when(has_up)
    def _():
        d_up.start()

    @pl.when(has_down)
    def _():
        d_down.start()

    put_acts(wide, act)
    receive(a_next, has_prev)
    put_acts(0, ahalo)
    temporal(acts, tf, pre, True)

    def out_row(n):
        h, f = pair(n)
        mix_ref[f, h] = x_ref[f, h] + pre[frame_rows(n, width)]

    each(strip * nf, out_row)
    start_z(0)

    def d_row(n):
        h, f = pair(n)
        put_row(ds, h + 1, f, dpre[h, frame_rows(f, width)])

    each(strip * nf, d_row)
    start_z(1)
    start_around(0)
    each(3, lambda i: put_weight(wb, i, jnp.concatenate([sw_ref[i, 2 - b].T for b in range(3)], axis=0)))
    start_around(1)
    start_back(0)
    start_back(1)
    receive(d_down, has_up)
    receive(d_up, has_down)

    def d_edge(n):
        side, f = pair(n)
        put_row(ds, side * (strip + 1), f, dhalo[side, frame_rows(f, width)])

    each(2 * nf, d_edge)
    conv(ds, wb, pre, True)

    def grad_row(n):
        h, f = pair(n)
        gi_ref[f, h] = cot_ref[f, h] + pre[frame_rows(n, width)]

    each(strip * nf, grad_row)
    for g in range(GROUPS):
        finish(g)

    for copy in sent:
        copy.wait_send()
    for copy, there in (
        (x_up, has_up), (x_down, has_down), (c_prev, has_prev),
        (a_next, has_next), (d_up, has_up), (d_down, has_down),
    ):
        pl.when(there)(copy.wait_send)


def write(share, mix_ref, gi_ref, gr_ref, out_ref, grad_ref, spatial_ref, temporal_ref, sem):
    pairs = [(mix_ref, out_ref), (gi_ref, grad_ref)]
    for tap in range(12):
        g, place = divmod(tap, 2 * PER_CORE)
        src = gr_ref.at[g, place // PER_CORE, pl.ds(place % PER_CORE * share, share)]
        pairs.append((src, temporal_ref.at[tap] if tap < 3 else spatial_ref.at[tap // 3 - 1, tap % 3]))
    copies = [pltpu.make_async_copy(src, dst, sem.at[n]) for n, (src, dst) in enumerate(pairs)]
    for copy in copies:
        copy.start()
    for copy in copies:
        copy.wait()


def per_device(nfd, nrd, images, spatial_weight, temporal_weight, cotangent):
    nf, strip, width, chans = images.shape
    wide, three = nf * width, 3 * chans
    nz, share = nfd // 2, chans // nrd
    piece = -(-(PER_CORE * share) // nz)
    piece = -(-piece // 8) * 8
    factor = 1.0 / math.sqrt(nf * nfd * strip * nrd * width)
    n_sems = 6 + GROUPS * (2 + (nrd - 1) + 2 * (nz - 1))
    vmem, hbm = (pl.BlockSpec(memory_space=space) for space in (pltpu.VMEM, pltpu.HBM))
    operands = (images, spatial_weight, temporal_weight, cotangent)
    operands = [pltpu.with_memory_space_constraint(a, pltpu.HBM) for a in operands]
    results = pl.pallas_call(
        functools.partial(kernel, nfd, nrd, share, piece, factor),
        out_shape=(
            pltpu.VMEM(images.shape, F32),
            pltpu.VMEM(images.shape, F32),
            pltpu.VMEM((GROUPS, 2, nz * piece, chans), F32),
        ),
        in_specs=[hbm] * 4,
        out_specs=(vmem,) * 3,
        scratch_shapes=[
            *(pltpu.VMEM(a.shape, F32) for a in operands),
            pltpu.SemaphoreType.DMA((4,)),
            pltpu.VMEM((strip * wide, chans), F32),
            pltpu.VMEM((strip * wide, chans), F32),
            pltpu.VMEM((2 * chans, strip * wide), BF16),
            pltpu.VMEM((2 * chans, strip * wide), BF16),
            pltpu.VMEM((2, strip + 2, wide, three), BF16),
            pltpu.VMEM((2, strip + 2, wide, three), BF16),
            pltpu.VMEM((3, three, 2 * chans), BF16),
            pltpu.VMEM((3, three, 2 * chans), BF16),
            pltpu.VMEM((3, chans, 2 * chans), BF16),
            pltpu.VMEM((3, chans, 2 * chans), BF16),
            pltpu.VMEM((2, nf, width, chans), F32),
            pltpu.VMEM((nf, strip, width, chans), F32),
            pltpu.VMEM((strip, wide, chans), F32),
            pltpu.VMEM((2, wide, chans), F32),
            pltpu.VMEM((strip, wide, chans), F32),
            pltpu.VMEM((strip, wide, chans), F32),
            pltpu.VMEM((2, strip, 2 * wide, chans), BF16),
            pltpu.VMEM((2, strip, 2 * wide, chans), BF16),
            pltpu.VMEM((12, chans, chans), F32),
            pltpu.VMEM((GROUPS, PER_CORE, chans, chans), F32),
            pltpu.VMEM((GROUPS, PER_CORE, chans, chans), F32),
            pltpu.VMEM((GROUPS, nrd - 1, PER_CORE, share, chans), F32),
            pltpu.VMEM((GROUPS, nz * piece, chans), F32),
            pltpu.VMEM((GROUPS, nz - 1, piece, chans), F32),
            pltpu.VMEM((GROUPS, 1, piece, chans), F32),
            pltpu.VMEM((GROUPS, 2, nz * piece, chans), F32),
            pltpu.SemaphoreType.DMA((n_sems,)),
            pltpu.SemaphoreType.DMA((n_sems,)),
        ],
        compiler_params=pltpu.CompilerParams(
            collective_id=0, has_side_effects=True, vmem_limit_bytes=VMEM_LIMIT
        ),
        cost_estimate=pl.CostEstimate(flops=1_400_000_000, bytes_accessed=2_000_000, transcendentals=50_000),
    )(*operands)
    out, gradient, spatial, temporal = pl.pallas_call(
        functools.partial(write, share),
        out_shape=(
            jax.ShapeDtypeStruct(images.shape, F32),
            jax.ShapeDtypeStruct(images.shape, F32),
            jax.ShapeDtypeStruct((3, 3, share, chans), F32),
            jax.ShapeDtypeStruct((3, share, chans), F32),
        ),
        in_specs=[vmem] * 3,
        out_specs=(hbm,) * 4,
        scratch_shapes=[pltpu.SemaphoreType.DMA((14,))],
        compiler_params=pltpu.CompilerParams(vmem_limit_bytes=VMEM_LIMIT),
        cost_estimate=pl.CostEstimate(flops=0, bytes_accessed=1_200_000, transcendentals=0),
    )(*results)
    return (
        out,
        gradient,
        spatial.transpose(0, 1, 3, 2),
        temporal.transpose(0, 2, 1),
    )


def solution(mesh):
    return jax.shard_map(
        functools.partial(per_device, mesh.shape["frames"], mesh.shape["rows"]),
        mesh=mesh,
        in_specs=(P("frames", "rows", None, None), P(), P(), P("frames", "rows", None, None)),
        out_specs=(
            P("frames", "rows", None, None),
            P("frames", "rows", None, None),
            P(None, None, None, "rows"),
            P(None, None, "rows"),
        ),
        check_vma=False,
    )
```
